256 devices in a mesh: gx: 32 (over z, y), gy: 8 (over x, core).
Axes of the slice: x: 4, y: 4, z: 8, core: 2. Of those that a mesh axis runs over, the one named last changes fastest.
Arguments:
- sources: bfloat16 [1, 64, 32, 64, 128], P(None, None, 'gx', 'gy'), may hold values from -6 to 6
- generator_weight: bfloat16 [3, 3, 3, 64, 64], replicated, may hold values from -0.4375 to 0.4375
- critic_kernel_weight: bfloat16 [3, 3, 3, 64, 64], replicated, may hold values from -0.15625 to 0.15625
- readout: float32 [64], replicated, may hold values from -1.5 to 1.5
- load_weight: int32 [32, 64], P('gx', 'gy'), may hold values from 1 to 8
Outputs:
- score: float32 [], replicated
- source_gradient: float32 [1, 64, 32, 64, 128], P(None, None, 'gx', 'gy')
- grad_gen: float32 [3, 3, 3, 64, 64], replicated
- grad_critic: float32 [3, 3, 3, 64, 64], replicated
The draws below stay inside these ranges and needn't reach their ends.
All inputs are finite; a program needn't handle non-finite values.
Results may differ from the reference program's by a relative error of at most 0.0043.
Values may be sent and summed in bfloat16 or wider, within the bound.
A program may use at most 128 MiB of HBM per device.

```python
import math
import jax
import jax.numpy as jnp
from jax import lax

C = 64
B = 1
NZ = 128
NX = 32
NY = 64
CELLS = 262144


def plant(drawn, own_key, smallest, high):
    spot = [jax.random.randint(jax.random.fold_in(own_key, axis), (), 0, length) for axis, length in enumerate(drawn.shape)]
    main_axis = drawn.shape.index(max(drawn.shape))
    beside = spot[:main_axis] + [(spot[main_axis] + 1) % drawn.shape[main_axis]] + spot[main_axis + 1:]
    return drawn.at[tuple(spot)].set(smallest).at[tuple(beside)].set(high)


def steps_of(key, dims, shards, low, largest):
    factor_of, own = 1.0, jax.random.fold_in(key, 6)
    for dim, parts in shards:
        heights = jnp.exp(jax.random.uniform(jax.random.fold_in(own, dim), (parts,), jnp.float32, low / len(shards), largest / len(shards)))
        factor_of = factor_of * jnp.repeat(heights, dims[dim] // parts).reshape([-1 if axis == dim else 1 for axis in range(len(dims))])
    return factor_of


def gaussian(key, extent, deviation, most, pieces=(), held_as=jnp.bfloat16):
    values = deviation * jax.random.normal(key, extent, jnp.float32)
    if pieces:
        values = values * steps_of(key, extent, pieces, -0.22, 0.18)
    return jnp.clip(values, -most, most).astype(held_as)


def setup_inputs(seed: int = 0) -> dict:
    arg_keys = jax.random.split(jax.random.key(seed), 6)
    return {
        "sources": gaussian(arg_keys[0], (B, C, NX, NY, NZ), 1.0, 6.0, ((2, 32), (3, 8))),
        "generator_weight": gaussian(arg_keys[1], (3, 3, 3, C, C), (27 * C // 8) ** -0.5, 0.4375),
        "critic_kernel_weight": gaussian(arg_keys[2], (3, 3, 3, C, C), (27 * C) ** -0.5, 0.15625),
        "readout": gaussian(arg_keys[3], (C,), (C // 4) ** -0.5, 1.5, (), jnp.float32),
        "load_weight": plant(jax.random.randint(arg_keys[4], (NX, NY), 1, 9), jax.random.fold_in(arg_keys[4], 1), 1, 8).astype(jnp.int32),
    }


DIMS_SPEC = ('NCDHW', 'DHWIO', 'NCDHW')
SWAP_SPEC = ('CNDHW', 'IODHW', 'NCDHW')
LOG_TWO = 0.6931471805599453

def activation(value):
    return 0.2 * value + 0.8 * (jax.nn.softplus(value) - LOG_TWO)

def act_slope(value):
    return 0.2 + 0.8 * jax.nn.sigmoid(value)

def upsample(source_field, kernel_taps, planar_padding):
    return lax.conv_general_dilated(source_field, jnp.flip(kernel_taps, (0, 1, 2)), (1, 1, 1), [planar_padding, planar_padding, (1, 2)], lhs_dilation=(2, 2, 2), dimension_numbers=DIMS_SPEC, preferred_element_type=jnp.float32)

def coarsen_field(source_field, kernel_taps, planar_padding):
    return lax.conv_general_dilated(source_field, kernel_taps, (2, 2, 2), [planar_padding, planar_padding, (1, 0)], dimension_numbers=DIMS_SPEC, preferred_element_type=jnp.float32)

def gen_taps(upper_box, grad_out):
    taps_out = lax.conv_general_dilated(grad_out, upper_box, (1, 1, 1), [(1, 2), (1, 2), (1, 0)], rhs_dilation=(2, 2, 2), dimension_numbers=SWAP_SPEC, preferred_element_type=jnp.float32)
    return jnp.transpose(taps_out, (2, 3, 4, 1, 0))

def critic_taps(lower_bounding_box, grad_out):
    taps_out = lax.conv_general_dilated(lower_bounding_box, grad_out, (1, 1, 1), [(0, 0), (0, 0), (1, 0)], rhs_dilation=(2, 2, 2), dimension_numbers=SWAP_SPEC, preferred_element_type=jnp.float32)
    return jnp.transpose(taps_out, (2, 3, 4, 0, 1))

def reference(sources, generator_weight, critic_kernel_weight, readout, load_weight):
    col_weight = load_weight.astype(jnp.float32)[None, :, :, None]
    read_col = readout[None, :, None, None, None]

    def one_sample(sample):
        source_one = sample[None]
        pre_gen = upsample(source_one, generator_weight, (1, 2))
        displacement_field = activation(pre_gen).astype(jnp.bfloat16)
        critic_preactivation = coarsen_field(displacement_field, critic_kernel_weight, (1, 0))
        logits = lax.optimization_barrier(jnp.sum(activation(critic_preactivation) * read_col, 1))
        loss_sum = jnp.sum(col_weight * jax.nn.softplus(-logits))
        d_logit = -col_weight * jax.nn.sigmoid(-logits)
        d_critic = (d_logit[:, None] * read_col * act_slope(critic_preactivation)).astype(jnp.bfloat16)
        lower_bounding_box = jnp.pad(displacement_field, ((0, 0), (0, 0), (1, 0), (1, 0), (0, 0)))
        crit_grad = critic_taps(lower_bounding_box, d_critic)
        d_field = upsample(d_critic, jnp.swapaxes(critic_kernel_weight, 3, 4), (1, 2))
        generator_gradient = (d_field * act_slope(pre_gen)).astype(jnp.bfloat16)
        upper_box = jnp.pad(source_one, ((0, 0), (0, 0), (0, 1), (0, 1), (0, 0)))
        gen_grad = gen_taps(upper_box, generator_gradient)
        input_gradient_part = coarsen_field(generator_gradient, jnp.swapaxes(generator_weight, 3, 4), (1, 0))[0]
        return (loss_sum, gen_grad, crit_grad, input_gradient_part)
    losses, gen_grads, crit_grads, source_gradient = lax.map(one_sample, sources)
    root = 1.0 / math.sqrt(CELLS)
    score = jnp.sum(losses) / CELLS
    return (score, source_gradient, lax.optimization_barrier(jnp.sum(gen_grads, 0)) * root, lax.optimization_barrier(jnp.sum(crit_grads, 0)) * root)
```

```python
import math

import jax
import jax.numpy as jnp
from jax import lax
from jax.experimental import pallas as pl
from jax.experimental.pallas import tpu as pltpu
from jax.sharding import PartitionSpec as P

MESH = pl.DeviceIdType.MESH
BF = jnp.bfloat16
F32 = jnp.float32
ROWS = 10
LANES = ROWS * 128
TILES = 14
TAP = {(0, 0): 1, (1, 0): 2, (1, 1): 0}
SIDES = [(1, 0), (-1, 0), (0, 1), (0, -1), (1, 1), (1, -1), (-1, 1), (-1, -1)]


def dot(a, b):
    return lax.dot_general(a, b, (((1,), (0,)), ((), ())), preferred_element_type=F32)


def dot_t(a, b):
    return lax.dot_general(a, b, (((1,), (1,)), ((), ())), preferred_element_type=F32)


def lane(shape):
    return lax.broadcasted_iota(jnp.int32, shape, len(shape) - 1)


def next_z(value):
    moved = pltpu.roll(value, 127, 1)
    return jnp.where(lane(value.shape) < 127, moved, 0.0)


def prev_z(value):
    moved = pltpu.roll(value, 1, 1)
    return jnp.where(lane(value.shape) > 0, moved, 0.0)


def at(row, count=1):
    return pl.ds(pl.multiple_of(row * 128, 128), count * 128)


def split_round(value, holds_loss):
    plain = value.astype(BF)
    loss = value[0:16] + value[16:32] + value[32:48]
    high = loss.astype(BF)
    rest = loss - high.astype(F32)
    middle = rest.astype(BF)
    low = (rest - middle.astype(F32)).astype(BF)
    parts = jnp.concatenate([high, middle, low, jnp.zeros_like(high)], 0).astype(F32)
    use = jnp.logical_and(lane(value.shape) >= 64, holds_loss)
    return jnp.where(use, parts, plain.astype(F32)).astype(BF)


def kernel(
    src_ref, wg_ref, wc_ref, ro_ref, lw_ref,
    score_ref, sg_ref, gg_ref, gc_ref,
    stage, sbuf, dbuf, wg, wgt, wc, wct, u, d, f, slope, dg, q, ro, lossv,
    part, core_rx, psend, plane_rx, z_rx, fin,
    s_s, s_r, d_s, d_r, csem, p_s, p_r, z_s, z_r, g_s, g_r, f_s, f_r,
):
    gx, gy = lax.axis_index("gx"), lax.axis_index("gy")
    z, y, x, core = gx // 4, gx % 4, gy // 2, gy % 2
    pme = x * 4 + y

    def plane_dev(p):
        return (z * 4 + p % 4, (p // 4) * 2 + core)

    def z_dev(t):
        return (t * 4 + y, gy)

    core_dev = (gx, x * 2 + (1 - core))

    def side_dev(side):
        return ((gx + side[0] + 32) % 32, (gy + side[1] + 8) % 8)

    def rcopy(src, dst, send, recv, dev):
        return pltpu.make_async_remote_copy(
            src_ref=src, dst_ref=dst, send_sem=send, recv_sem=recv, device_id=dev, device_id_type=MESH
        )

    def halo(buf, n, send, recv):
        dx, dy = SIDES[n]
        here = pl.ds(1, 8) if dy == 0 else pl.ds(8 if dy > 0 else 1, 1)
        there = pl.ds(1, 8) if dy == 0 else pl.ds(0 if dy > 0 else 9, 1)
        return rcopy(buf.at[1, here], buf.at[1 - dx, there], send.at[n], recv.at[n], side_dev(SIDES[n]))

    barrier = pltpu.get_barrier_semaphore()

    def greet(dev):
        pl.semaphore_signal(barrier, inc=1, device_id=dev, device_id_type=MESH)

    for side in SIDES:
        greet(side_dev(side))
    greet(core_dev)

    @pl.loop(1, 16)
    def _(t):
        greet(plane_dev((pme + t) % 16))

    @pl.loop(1, 8)
    def _(t):
        greet(z_dev((z + t) % 8))

    stage[...] = src_ref[...].astype(F32)
    for r in range(8):
        sbuf[1, r + 1] = stage[:, r, :].astype(BF)

    pl.semaphore_wait(barrier, 8 + 1 + 15 + 7)
    for n in range(8):
        halo(sbuf, n, s_s, s_r).start()

    zero = jnp.zeros((64, 64), F32)
    for s in range(3):
        for ay in range(2):
            for az in range(2):
                rows = pl.ds((ay * 2 + az) * 64, 64)
                for by in range(2):
                    pair = []
                    for bz in range(2):
                        ok = (by, ay) in TAP and (bz, az) in TAP
                        pair.append(wg_ref[s * 9 + TAP[by, ay] * 3 + TAP[bz, az]].astype(F32) if ok else zero)
                    wg[s, rows, pl.ds(by * 128, 128)] = jnp.concatenate(pair, 1).astype(BF)
                    pair = []
                    for bz in range(2):
                        ok = (ay, by) in TAP and (az, bz) in TAP
                        pair.append(wc_ref[s * 9 + TAP[ay, by] * 3 + TAP[az, bz]].astype(F32) if ok else zero)
                    wc[s, rows, pl.ds(by * 128, 128)] = jnp.concatenate(pair, 1).astype(BF)
        wgt[s] = wg[s].astype(F32).T.astype(BF)
        wct[s] = wc[s].astype(F32).T.astype(BF)
    ro[...] = jnp.broadcast_to(ro_ref[...], (128, 64)).T

    def spread(buf, out, xs, r, keep=None):
        value = buf[xs, r].astype(F32)
        if keep is not None:
            value = jnp.where(keep, value, 0.0)
        return value.astype(BF), next_z(value).astype(BF)

    def put_here(out, xs, r, pair):
        out[xs, 0:64, at(r)] = pair[0]
        out[xs, 64:128, at(r)] = pair[1]

    def put_below(out, xs, r, pair):
        out[xs, 128:192, at(r - 1)] = pair[0]
        out[xs, 192:256, at(r - 1)] = pair[1]

    def clear(out, xs):
        nothing = jnp.zeros((128, 128), BF)
        out[xs, 0:128, at(0)] = nothing
        out[xs, 0:128, at(9)] = nothing
        out[xs, 128:256, at(8)] = nothing
        out[xs, 128:256, at(9)] = nothing

    def own_rows(buf, out, xs, keep=None):
        @pl.loop(1, 9)
        def _(r):
            pair = spread(buf, out, xs, r, keep)
            put_here(out, xs, r, pair)
            put_below(out, xs, r, pair)

    def edge_rows(buf, out, xs, keep=True):
        put_here(out, xs, 0, spread(buf, out, xs, 0, keep))
        put_below(out, xs, 9, spread(buf, out, xs, 9, jnp.logical_and(keep, gy < 7)))

    clear(u, 1)
    own_rows(sbuf, u, 1)
    clear(d, 1)

    for n in range(8):
        halo(sbuf, n, s_s, s_r).wait_recv()
    for xs in (0, 2):
        clear(u, xs)
    edge_rows(sbuf, u, 1)
    own_rows(sbuf, u, 0)
    edge_rows(sbuf, u, 0)
    own_rows(sbuf, u, 2, gx < 31)
    edge_rows(sbuf, u, 2, gx < 31)

    def up(weights, field, c):
        mid = field[1, :, c]
        return (
            dot(weights[2], field[0, :, c]) + dot(weights[0], mid),
            dot(weights[1], mid),
            dot(weights[2], mid) + dot(weights[0], field[2, :, c]),
        )

    @pl.loop(0, ROWS // 2)
    def _(i):
        c = at(i * 2, 2)
        for s, v in enumerate(up(wgt, u, c)):
            t = jnp.tanh(0.5 * v)
            f[s, :, c] = (jnp.maximum(v, 0.2 * v) - 0.8 * jnp.log(1.0 + jnp.abs(t))).astype(BF)
            slope[s, :, c] = 0.6 + 0.4 * t

    @pl.when(gx == 0)
    def _():
        f[0] = jnp.zeros((256, LANES), BF)
        slope[0] = jnp.zeros((256, LANES), F32)

    @pl.when(gy == 0)
    def _():
        for s in range(3):
            f[s, :, 0:128] = jnp.zeros((256, 128), BF)
            slope[s, :, 0:128] = jnp.zeros((256, 128), F32)

    def down(weights, field, c):
        return dot(weights[0], field[0, :, c]) + dot(weights[1], field[1, :, c]) + dot(weights[2], field[2, :, c])

    def gathered(r):
        near = q[0:64, at(r)] + q[128:192, at(r - 1)]
        far = q[64:128, at(r)] + q[192:256, at(r - 1)]
        return near + prev_z(far)

    @pl.loop(0, ROWS // 2)
    def _(i):
        c = at(i * 2, 2)
        q[:, c] = down(wct, f, c)

    lossv[...] = jnp.zeros((1, 128), F32)

    @pl.loop(1, 9)
    def _(r):
        v = gathered(r)
        t = jnp.tanh(0.5 * v)
        act = jnp.maximum(v, 0.2 * v) - 0.8 * jnp.log(1.0 + jnp.abs(t))
        logits = jnp.sum(act * ro[...], 0, keepdims=True)
        weight = lw_ref[0, r - 1].astype(F32)
        e = jnp.exp(-jnp.abs(logits))
        lossv[...] += weight * (jnp.maximum(-logits, 0.0) + jnp.log1p(e))
        d_logit = -weight * jnp.where(logits >= 0, e, 1.0) / (1.0 + e)
        dbuf[1, r] = (d_logit * ro[...] * (0.6 + 0.4 * t)).astype(BF)

    for n in range(8):
        halo(dbuf, n, d_s, d_r).start()
    own_rows(dbuf, d, 1)

    def pack(g, s, full, halves):
        for j in range(3):
            n = s * 3 + j
            part[g, n] = full[j]
            left = lane((64, 128)) < 64
            half = halves[j]
            if (g == 0) == (n % 2 == 1):
                half = pltpu.roll(half, 64, 1)
            if n % 2 == 0:
                part[g, 9 + n // 2] = jnp.where(left, half, 0.0)
            else:
                part[g, 9 + n // 2] = jnp.where(left, part[g, 9 + n // 2], half)

    for s in range(3):
        q[:, 0:256] = dot_t(f[s], d[1])
        pairs = [(0, 0), (1, 0), (1, 1)]
        pack(
            0, s,
            [q[(p * 2 + 1) * 64:(p * 2 + 2) * 64, e * 128:e * 128 + 128] for p, e in pairs],
            [q[p * 128:p * 128 + 64, e * 128:e * 128 + 128] for p, e in pairs],
        )
    loss = jnp.broadcast_to(jnp.sum(lossv[...], 1, keepdims=True), (16, 128))
    put = lane((16, 128)) >= 64
    part[0, 13, 0:16, :] = jnp.where(put, loss, part[0, 13, 0:16, :])

    for n in range(8):
        halo(dbuf, n, d_s, d_r).wait_recv()
    for xs in (0, 2):
        clear(d, xs)
    edge_rows(dbuf, d, 1)
    own_rows(dbuf, d, 0)
    edge_rows(dbuf, d, 0)
    own_rows(dbuf, d, 2, gx < 31)
    edge_rows(dbuf, d, 2, gx < 31)

    @pl.loop(0, ROWS // 2)
    def _(i):
        c = at(i * 2, 2)
        for s, v in enumerate(up(wc, d, c)):
            dg[s, :, c] = (v * slope[s, :, c]).astype(BF)

    clear(u, 1)
    for s in range(3):
        q[:, 0:256] = dot_t(u[1], dg[s])
        pairs = [(0, 0), (0, 1), (1, 1)]
        pack(
            1, s,
            [q[e * 128:e * 128 + 64, p * 128:p * 128 + 128] for e, p in pairs],
            [q[e * 128 + 64:e * 128 + 128, p * 128:p * 128 + 128] for e, p in pairs],
        )

    pair = rcopy(part.at[1 - core], core_rx, csem.at[0], csem.at[1], core_dev)
    pair.start()
    for n in range(8):
        halo(sbuf, n, s_s, s_r).wait_send()
        halo(dbuf, n, d_s, d_r).wait_send()
    pair.wait()

    def loss_tile(t):
        return jnp.logical_and(core == 0, t == 13)

    def to_owner(dst, src):
        return rcopy(psend.at[dst], plane_rx.at[src], p_s.at[dst], p_r.at[src], plane_dev(dst))

    @pl.loop(1, 17)
    def _(i):
        t = (pme + i) % 16

        @pl.when(t < TILES)
        def _():
            psend[t] = split_round(part[core, t] + core_rx[t], loss_tile(t))

            @pl.when(t != pme)
            def _():
                to_owner(t, pme).start()

    @pl.loop(0, ROWS // 2)
    def _(i):
        c = at(i * 2, 2)
        q[:, c] = down(wg, dg, c)

    @pl.loop(1, 9)
    def _(r):
        sg_ref[r - 1] = gathered(r)

    def along_z(dst, src):
        return rcopy(z_rx.at[src], z_rx.at[src], z_s.at[dst], z_r.at[src], z_dev(dst))

    def to_plane(dst, src):
        return rcopy(fin.at[core, src], fin.at[core, src], g_s.at[dst], g_r.at[src], plane_dev(dst))

    def to_core(g, t):
        return rcopy(fin.at[g, t], fin.at[g, t], f_s.at[t], f_r.at[t], core_dev)

    @pl.when(pme < TILES)
    def _():
        plane_rx[pme] = psend[pme]

        @pl.loop(1, 16)
        def _(i):
            t = (pme + i) % 16
            to_owner(pme, t).wait_recv()

        total = plane_rx[0].astype(F32)
        for t in range(1, 16):
            total += plane_rx[t].astype(F32)
        z_rx[z] = split_round(total, loss_tile(pme))

        @pl.loop(1, 8)
        def _(i):
            along_z((z + i) % 8, z).start()

        @pl.loop(1, 8)
        def _(i):
            t = (z + i) % 8
            along_z(t, t).wait_recv()

        total = z_rx[0].astype(F32)
        for t in range(1, 8):
            total += z_rx[t].astype(F32)
        fin[core, pme] = split_round(total, loss_tile(pme))
        to_core(core, pme).start()

        @pl.loop(1, 16)
        def _(i):
            to_plane((pme + i) % 16, pme).start()

    @pl.loop(1, 16)
    def _(i):
        t = (pme + 16 - i) % 16

        @pl.when(t < TILES)
        def _():
            to_plane(pme, t).wait_recv()
            to_core(core, t).start()

    @pl.loop(0, TILES)
    def _(t):
        to_core(1 - core, t).wait_recv()

    root = 1.0 / math.sqrt(262144.0)
    for g, out, full_taps, half_tap in ((0, gc_ref, (2, 0), 1), (1, gg_ref, (1, 2), 0)):
        for n in range(9):
            first = (n // 3) * 9 + (1, 2, 0)[n % 3] * 3
            full = fin[g, n].astype(F32) * root
            out[first + full_taps[0]] = full[:, 0:64]
            out[first + full_taps[1]] = full[:, 64:128]
            half = fin[g, 9 + n // 2].astype(F32) * root
            out[first + half_tap] = half[:, 0:64] if n % 2 == 0 else half[:, 64:128]
    loss = fin[0, 13].astype(F32)
    loss = loss[0:16] + loss[16:32] + loss[32:48]
    score_ref[0, 0] = jnp.sum(jnp.where(jnp.logical_and(lane((16, 128)) == 64, lax.broadcasted_iota(jnp.int32, (16, 128), 0) == 0), loss, 0.0)) * (1.0 / 262144.0)

    @pl.loop(1, 16)
    def _(i):
        t = (pme + i) % 16

        @pl.when(t < TILES)
        def _():
            to_owner(t, pme).wait_send()

    @pl.when(pme < TILES)
    def _():
        @pl.loop(1, 8)
        def _(i):
            along_z((z + i) % 8, z).wait_send()

        @pl.loop(1, 16)
        def _(i):
            to_plane((pme + i) % 16, pme).wait_send()

    @pl.loop(0, TILES)
    def _(t):
        to_core(core, t).wait_send()


def shards(sources, generator_weight, critic_kernel_weight, readout, load_weight):
    vmem = pl.BlockSpec(memory_space=pltpu.VMEM)
    smem = pl.BlockSpec(memory_space=pltpu.SMEM)
    dma = pltpu.SemaphoreType.DMA
    score, source_gradient, gen, crit = pl.pallas_call(
        kernel,
        out_shape=(
            jax.ShapeDtypeStruct((1, 1), F32),
            jax.ShapeDtypeStruct((8, 64, 128), F32),
            jax.ShapeDtypeStruct((27, 64, 64), F32),
            jax.ShapeDtypeStruct((27, 64, 64), F32),
        ),
        in_specs=[vmem, vmem, vmem, vmem, smem],
        out_specs=(smem, vmem, vmem, vmem),
        scratch_shapes=[
            pltpu.VMEM((64, 8, 128), F32),
            pltpu.VMEM((3, ROWS, 64, 128), BF),
            pltpu.VMEM((3, ROWS, 64, 128), BF),
            pltpu.VMEM((3, 256, 256), BF),
            pltpu.VMEM((3, 256, 256), BF),
            pltpu.VMEM((3, 256, 256), BF),
            pltpu.VMEM((3, 256, 256), BF),
            pltpu.VMEM((3, 256, LANES), BF),
            pltpu.VMEM((3, 256, LANES), BF),
            pltpu.VMEM((3, 256, LANES), BF),
            pltpu.VMEM((3, 256, LANES), F32),
            pltpu.VMEM((3, 256, LANES), BF),
            pltpu.VMEM((256, LANES), F32),
            pltpu.VMEM((64, 128), F32),
            pltpu.VMEM((1, 128), F32),
            pltpu.VMEM((2, TILES, 64, 128), F32),
            pltpu.VMEM((TILES, 64, 128), F32),
            pltpu.VMEM((TILES, 64, 128), BF),
            pltpu.VMEM((16, 64, 128), BF),
            pltpu.VMEM((8, 64, 128), BF),
            pltpu.VMEM((2, TILES, 64, 128), BF),
            dma((8,)), dma((8,)), dma((8,)), dma((8,)), dma((2,)),
            dma((TILES,)), dma((16,)), dma((8,)), dma((8,)),
            dma((16,)), dma((TILES,)), dma((TILES,)), dma((TILES,)),
        ],
        compiler_params=pltpu.CompilerParams(
            collective_id=0, has_side_effects=True, vmem_limit_bytes=56 * 2**20
        ),
        cost_estimate=pl.CostEstimate(flops=3 * 10**9, bytes_accessed=4 * 10**6, transcendentals=2 * 10**6),
    )(
        sources.reshape(64, 8, 128),
        generator_weight.reshape(27, 64, 64),
        critic_kernel_weight.reshape(27, 64, 64),
        readout.reshape(1, 64),
        load_weight,
    )
    return (
        score.reshape(()),
        jnp.swapaxes(source_gradient, 0, 1).reshape(1, 64, 1, 8, 128),
        gen.reshape(3, 3, 3, 64, 64),
        crit.reshape(3, 3, 3, 64, 64),
    )


def solution(mesh):
    placed = (P(None, None, "gx", "gy", None), P(), P(), P(), P("gx", "gy"))
    return jax.shard_map(
        shards,
        mesh=mesh,
        in_specs=placed,
        out_specs=(P(), P(None, None, "gx", "gy", None), P(), P()),
        check_vma=False,
    )
```

```python
import math

import jax
import jax.numpy as jnp
from jax import lax
from jax.experimental import pallas as pl
from jax.experimental.pallas import tpu as pltpu
from jax.sharding import PartitionSpec as P

MESH = pl.DeviceIdType.MESH
BF = jnp.bfloat16
F32 = jnp.float32
ROWS = 9
LANES = ROWS * 128
TILES = 14
TAP = {(0, 0): 1, (1, 0): 2, (1, 1): 0}
SIDES = [(1, 0), (-1, 0), (0, 1), (0, -1), (1, 1), (1, -1), (-1, 1), (-1, -1)]


def dot(a, b):
    return lax.dot_general(a, b, (((1,), (0,)), ((), ())), preferred_element_type=F32)


def dot_t(a, b):
    return lax.dot_general(a, b, (((1,), (1,)), ((), ())), preferred_element_type=F32)


def lane(shape):
    return lax.broadcasted_iota(jnp.int32, shape, len(shape) - 1)


def next_z(value):
    moved = pltpu.roll(value, 127, 1)
    return jnp.where(lane(value.shape) < 127, moved, 0.0)


def prev_z(value):
    moved = pltpu.roll(value, 1, 1)
    return jnp.where(lane(value.shape) > 0, moved, 0.0)


def at(row, count=1):
    return pl.ds(pl.multiple_of(row * 128, 128), count * 128)


def split_round(value, holds_loss):
    plain = value.astype(BF)
    loss = value[0:16] + value[16:32] + value[32:48]
    high = loss.astype(BF)
    rest = loss - high.astype(F32)
    middle = rest.astype(BF)
    low = (rest - middle.astype(F32)).astype(BF)
    parts = jnp.concatenate([high, middle, low, jnp.zeros_like(high)], 0).astype(F32)
    use = jnp.logical_and(lane(value.shape) >= 64, holds_loss)
    return jnp.where(use, parts, plain.astype(F32)).astype(BF)


def kernel(
    src_hbm, wg_hbm, wc_hbm, ro_hbm, lw_ref,
    sg_ref, fin,
    src_ref, wg_ref, wc_ref, ro_ref, lsem, half_field, stage, sbuf, dbuf, wg, wgt, wc, wct, u, d, f, slope, dg, q, ro, lossv,
    part, core_rx, psend, plane_rx, z_rx,
    s_s, s_r, d_s, d_r, csem, p_s, p_r, z_s, z_r, g_s, g_r, f_s, f_r,
):
    gx, gy = lax.axis_index("gx"), lax.axis_index("gy")
    z, y, x, core = gx // 4, gx % 4, gy // 2, gy % 2
    pme = x * 4 + y

    def plane_dev(p):
        return (z * 4 + p % 4, (p // 4) * 2 + core)

    def z_dev(t):
        return (t * 4 + y, gy)

    core_dev = (gx, x * 2 + (1 - core))

    def side_dev(side):
        return ((gx + side[0] + 32) % 32, (gy + side[1] + 8) % 8)

    def rcopy(src, dst, send, recv, dev):
        return pltpu.make_async_remote_copy(
            src_ref=src, dst_ref=dst, send_sem=send, recv_sem=recv, device_id=dev, device_id_type=MESH
        )

    def halo(buf, n, send, recv, half=0):
        dx, dy = SIDES[n]
        if dy == 0:
            here = there = pl.ds(1 + 4 * half, 4)
        else:
            here, there = pl.ds(8 if dy > 0 else 1, 1), pl.ds(0 if dy > 0 else 9, 1)
        n = n + 8 * half
        return rcopy(buf.at[1, here], buf.at[1 - dx, there], send.at[n], recv.at[n], side_dev((dx, dy)))

    loads = [
        pltpu.make_async_copy(a, b, lsem.at[n])
        for n, (a, b) in enumerate(((src_hbm, src_ref), (wg_hbm, wg_ref), (wc_hbm, wc_ref), (ro_hbm, ro_ref)))
    ]
    for load in loads:
        load.start()

    barrier = pltpu.get_barrier_semaphore()

    def greet(dev):
        pl.semaphore_signal(barrier, inc=1, device_id=dev, device_id_type=MESH)

    for side in SIDES:
        greet(side_dev(side))
    greet(core_dev)

    @pl.loop(1, 16)
    def _(t):
        greet(plane_dev((pme + t) % 16))

    @pl.loop(1, 8)
    def _(t):
        greet(z_dev((z + t) % 8))

    loads[0].wait()
    stage[...] = src_ref[...].astype(F32)
    for r in range(8):
        sbuf[1, r + 1] = stage[:, r, :].astype(BF)

    pl.semaphore_wait(barrier, 8 + 1 + 15 + 7)
    parts = [(0, 0), (1, 0), (0, 1), (1, 1)] + [(n, 0) for n in range(2, 8)]
    for n, half in parts:
        halo(sbuf, n, s_s, s_r, half).start()
    for load in loads[1:]:
        load.wait()

    zero = jnp.zeros((64, 64), F32)
    for s in range(3):
        for ay in range(2):
            for az in range(2):
                rows = pl.ds((ay * 2 + az) * 64, 64)
                for by in range(2):
                    pair = []
                    for bz in range(2):
                        ok = (by, ay) in TAP and (bz, az) in TAP
                        pair.append(wg_ref[s * 9 + TAP[by, ay] * 3 + TAP[bz, az]].astype(F32) if ok else zero)
                    wg[s, rows, pl.ds(by * 128, 128)] = jnp.concatenate(pair, 1).astype(BF)
                    pair = []
                    for bz in range(2):
                        ok = (ay, by) in TAP and (az, bz) in TAP
                        pair.append(wc_ref[s * 9 + TAP[ay, by] * 3 + TAP[az, bz]].astype(F32) if ok else zero)
                    wc[s, rows, pl.ds(by * 128, 128)] = jnp.concatenate(pair, 1).astype(BF)
        wgt[s] = wg[s].astype(F32).T.astype(BF)
        wct[s] = wc[s].astype(F32).T.astype(BF)
    ro[...] = jnp.broadcast_to(ro_ref[...], (128, 64)).T

    def spread(buf, out, xs, r, keep=None):
        value = buf[xs, r].astype(F32)
        if keep is not None:
            value = jnp.where(keep, value, 0.0)
        return value.astype(BF), next_z(value).astype(BF)

    def put_here(out, xs, r, pair):
        out[xs, 0:64, at(r)] = pair[0]
        out[xs, 64:128, at(r)] = pair[1]

    def put_below(out, xs, r, pair):
        out[xs, 128:192, at(r - 1)] = pair[0]
        out[xs, 192:256, at(r - 1)] = pair[1]

    def clear(out, xs):
        nothing = jnp.zeros((128, 128), BF)
        out[xs, 0:128, at(0)] = nothing
        out[xs, 128:256, at(8)] = nothing

    def own_rows(buf, out, xs, keep=None):
        @pl.loop(1, 9, unroll=4)
        def _(r):
            pair = spread(buf, out, xs, r, keep)
            put_here(out, xs, r, pair)
            put_below(out, xs, r, pair)

    def edge_rows(buf, out, xs, keep=True):
        put_here(out, xs, 0, spread(buf, out, xs, 0, keep))
        put_below(out, xs, 9, spread(buf, out, xs, 9, jnp.logical_and(keep, gy < 7)))

    clear(u, 1)
    own_rows(sbuf, u, 1)
    clear(d, 1)

    def fire(s, v, c):
        t = jnp.tanh(0.5 * v)
        f[s, :, c] = (jnp.maximum(v, 0.2 * v) - 0.8 * jnp.log(1.0 + jnp.abs(t))).astype(BF)
        slope[s, :, c] = 0.6 + 0.4 * t

    def fire_low(s, v):
        t = jnp.tanh(0.5 * v)
        f[s, 128:256, 0:128] = (jnp.maximum(v, 0.2 * v) - 0.8 * jnp.log(1.0 + jnp.abs(t))).astype(BF)
        slope[s, 128:256, 0:128] = 0.6 + 0.4 * t

    def up_mid(weights, field, c):
        mid = field[1, :, c]
        return dot(weights[0], mid), dot(weights[1], mid), dot(weights[2], mid)

    def up_rest(weights, field, c):
        return dot(weights[2], field[0, :, c]), dot(weights[0], field[2, :, c])

    def up_low(weights, field):
        below, mid, above = field[0, :, 0:128], field[1, :, 0:128], field[2, :, 0:128]
        w0, w1, w2 = (weights[k, 128:256, :] for k in range(3))
        return dot(w2, below) + dot(w0, mid), dot(w1, mid), dot(w2, mid) + dot(w0, above)

    @pl.loop(0, 3)
    def _(j):
        c = at(j * 2 + 1, 2)
        low, mid, high = up_mid(wgt, u, c)
        fire(1, mid, c)
        slope[0, :, c] = low
        slope[2, :, c] = high

    for s in range(3):
        f[s, 0:128, 0:128] = jnp.zeros((128, 128), BF)
        dg[s, 0:128, 0:128] = jnp.zeros((128, 128), BF)

    for n, half in parts:
        halo(sbuf, n, s_s, s_r, half).wait_recv()
    for xs in (0, 2):
        clear(u, xs)
    edge_rows(sbuf, u, 1)
    own_rows(sbuf, u, 0)
    edge_rows(sbuf, u, 0)
    own_rows(sbuf, u, 2, gx < 31)
    edge_rows(sbuf, u, 2, gx < 31)

    for s, v in enumerate(up_low(wgt, u)):
        fire_low(s, v)
    c = at(7, 2)
    low, mid, high = up_mid(wgt, u, c)
    fire(1, mid, c)
    slope[0, :, c] = low
    slope[2, :, c] = high

    @pl.loop(0, 4)
    def _(j):
        c = at(j * 2 + 1, 2)
        low, high = up_rest(wgt, u, c)
        fire(0, slope[0, :, c] + low, c)
        fire(2, slope[2, :, c] + high, c)

    @pl.when(gx == 0)
    def _():
        f[0] = jnp.zeros((256, LANES), BF)
        slope[0] = jnp.zeros((256, LANES), F32)

    @pl.when(gy == 0)
    def _():
        for s in range(3):
            f[s, 128:256, 0:128] = jnp.zeros((128, 128), BF)
            slope[s, 128:256, 0:128] = jnp.zeros((128, 128), F32)

    def down(weights, field, c):
        return dot(weights[0], field[0, :, c]) + dot(weights[1], field[1, :, c]) + dot(weights[2], field[2, :, c])

    def down_low(weights, field):
        terms = [dot(weights[k, 128:256, 128:256], field[k, 128:256, 0:128]) for k in range(3)]
        return terms[0] + terms[1] + terms[2]

    def gathered(r):
        near = q[0:64, at(r)] + q[128:192, at(r - 1)]
        far = q[64:128, at(r)] + q[192:256, at(r - 1)]
        return near + prev_z(far)

    q[128:256, 0:128] = down_low(wct, f)
    lossv[...] = jnp.zeros((1, 128), F32)

    def judge(r):
        v = gathered(r)
        t = jnp.tanh(0.5 * v)
        act = jnp.maximum(v, 0.2 * v) - 0.8 * jnp.log(1.0 + jnp.abs(t))
        logits = jnp.sum(act * ro[...], 0, keepdims=True)
        weight = lw_ref[0, r - 1].astype(F32)
        e = jnp.exp(-jnp.abs(logits))
        lossv[...] += weight * (jnp.maximum(-logits, 0.0) + jnp.log1p(e))
        d_logit = -weight * jnp.where(logits >= 0, e, 1.0) / (1.0 + e)
        dbuf[1, r] = (d_logit * ro[...] * (0.6 + 0.4 * t)).astype(BF)

    for half in range(2):
        @pl.loop(2 * half, 2 * half + 2)
        def _(j):
            c = at(j * 2 + 1, 2)
            q[:, c] = down(wct, f, c)
            judge(2 * j + 1)
            judge(2 * j + 2)

        for n in (0, 1):
            halo(dbuf, n, d_s, d_r, half).start()
        for n in (3, 5, 7) if half == 0 else (2, 4, 6):
            halo(dbuf, n, d_s, d_r).start()
    own_rows(dbuf, d, 1)

    @pl.loop(0, 3)
    def _(j):
        c = at(j * 2 + 1, 2)
        low, mid, high = up_mid(wc, d, c)
        dg[1, :, c] = (mid * slope[1, :, c]).astype(BF)
        half_field[0, :, c] = low
        half_field[1, :, c] = high

    def pack(g, s, full, halves):
        for j in range(3):
            n = s * 3 + j
            part[g, n] = full[j]
            left = lane((64, 128)) < 64
            half = halves[j]
            if (g == 0) == (n % 2 == 1):
                half = pltpu.roll(half, 64, 1)
            if n % 2 == 0:
                part[g, 9 + n // 2] = jnp.where(left, half, 0.0)
            else:
                part[g, 9 + n // 2] = jnp.where(left, part[g, 9 + n // 2], half)

    for s in range(3):
        q[:, 0:256] = dot_t(f[s], d[1])
        pairs = [(0, 0), (1, 0), (1, 1)]
        pack(
            0, s,
            [q[(p * 2 + 1) * 64:(p * 2 + 2) * 64, e * 128:e * 128 + 128] for p, e in pairs],
            [q[p * 128:p * 128 + 64, e * 128:e * 128 + 128] for p, e in pairs],
        )
    loss = jnp.broadcast_to(jnp.sum(lossv[...], 1, keepdims=True), (16, 128))
    put = lane((16, 128)) >= 64
    part[0, 13, 0:16, :] = jnp.where(put, loss, part[0, 13, 0:16, :])

    for n, half in parts:
        halo(dbuf, n, d_s, d_r, half).wait_recv()
    for xs in (0, 2):
        clear(d, xs)
    edge_rows(dbuf, d, 1)
    own_rows(dbuf, d, 0)
    edge_rows(dbuf, d, 0)
    own_rows(dbuf, d, 2, gx < 31)
    edge_rows(dbuf, d, 2, gx < 31)

    for s, v in enumerate(up_low(wc, d)):
        dg[s, 128:256, 0:128] = (v * slope[s, 128:256, 0:128]).astype(BF)
    c = at(7, 2)
    low, mid, high = up_mid(wc, d, c)
    dg[1, :, c] = (mid * slope[1, :, c]).astype(BF)
    half_field[0, :, c] = low
    half_field[1, :, c] = high

    @pl.loop(0, 4)
    def _(j):
        c = at(j * 2 + 1, 2)
        low, high = up_rest(wc, d, c)
        dg[0, :, c] = ((half_field[0, :, c] + low) * slope[0, :, c]).astype(BF)
        dg[2, :, c] = ((half_field[1, :, c] + high) * slope[2, :, c]).astype(BF)

    clear(u, 1)
    for s in range(3):
        q[:, 0:256] = dot_t(u[1], dg[s])
        pairs = [(0, 0), (0, 1), (1, 1)]
        pack(
            1, s,
            [q[e * 128:e * 128 + 64, p * 128:p * 128 + 128] for e, p in pairs],
            [q[e * 128 + 64:e * 128 + 128, p * 128:p * 128 + 128] for e, p in pairs],
        )

    pair = rcopy(part.at[1 - core], core_rx, csem.at[0], csem.at[1], core_dev)
    pair.start()
    for n, half in parts:
        halo(sbuf, n, s_s, s_r, half).wait_send()
        halo(dbuf, n, d_s, d_r, half).wait_send()
    pair.wait()

    def loss_tile(t):
        return jnp.logical_and(core == 0, t == 13)

    def to_owner(dst, src):
        return rcopy(psend.at[dst], plane_rx.at[src], p_s.at[dst], p_r.at[src], plane_dev(dst))

    @pl.loop(1, 17)
    def _(i):
        t = (pme + i) % 16

        @pl.when(t < TILES)
        def _():
            psend[t] = split_round(part[core, t] + core_rx[t], loss_tile(t))

            @pl.when(t != pme)
            def _():
                to_owner(t, pme).start()

    q[128:256, 0:128] = down_low(wg, dg)

    @pl.loop(0, 4)
    def _(j):
        c = at(j * 2 + 1, 2)
        q[:, c] = down(wg, dg, c)
        sg_ref[2 * j] = gathered(2 * j + 1)
        sg_ref[2 * j + 1] = gathered(2 * j + 2)

    def along_z(dst, src):
        return rcopy(z_rx.at[src], z_rx.at[src], z_s.at[dst], z_r.at[src], z_dev(dst))

    def to_plane(dst, src):
        return rcopy(fin.at[core, src], fin.at[core, src], g_s.at[dst], g_r.at[src], plane_dev(dst))

    def to_core(g, t):
        return rcopy(fin.at[g, t], fin.at[g, t], f_s.at[t], f_r.at[t], core_dev)

    @pl.when(pme < TILES)
    def _():
        plane_rx[pme] = psend[pme]

        @pl.loop(1, 16)
        def _(i):
            t = (pme + i) % 16
            to_owner(pme, t).wait_recv()

        total = plane_rx[0].astype(F32)
        for t in range(1, 16):
            total += plane_rx[t].astype(F32)
        z_rx[z] = split_round(total, loss_tile(pme))

        @pl.loop(1, 8)
        def _(i):
            along_z((z + i) % 8, z).start()

        @pl.loop(1, 8)
        def _(i):
            t = (z + i) % 8
            along_z(t, t).wait_recv()

        total = z_rx[0].astype(F32)
        for t in range(1, 8):
            total += z_rx[t].astype(F32)
        fin[core, pme] = split_round(total, loss_tile(pme))
        to_core(core, pme).start()

        @pl.loop(1, 16)
        def _(i):
            to_plane((pme + i) % 16, pme).start()

    @pl.loop(1, 16)
    def _(i):
        t = (pme + 16 - i) % 16

        @pl.when(t < TILES)
        def _():
            to_plane(pme, t).wait_recv()
            to_core(core, t).start()

    @pl.loop(0, TILES)
    def _(t):
        to_core(1 - core, t).wait_recv()

    @pl.loop(1, 16)
    def _(i):
        t = (pme + i) % 16

        @pl.when(t < TILES)
        def _():
            to_owner(t, pme).wait_send()

    @pl.when(pme < TILES)
    def _():
        @pl.loop(1, 8)
        def _(i):
            along_z((z + i) % 8, z).wait_send()

        @pl.loop(1, 16)
        def _(i):
            to_plane((pme + i) % 16, pme).wait_send()

    @pl.loop(0, TILES)
    def _(t):
        to_core(core, t).wait_send()


def unpack(fin, sg_ref, score_ref, sgo_ref, gg_ref, gc_ref):
    for r in range(8):
        sgo_ref[:, r, :] = sg_ref[r]
    root = 1.0 / math.sqrt(262144.0)
    for g, out, full_taps, half_tap in ((0, gc_ref, (2, 0), 1), (1, gg_ref, (1, 2), 0)):
        for n in range(9):
            first = (n // 3) * 9 + (1, 2, 0)[n % 3] * 3
            full = fin[g, n].astype(F32) * root
            out[first + full_taps[0]] = full[:, 0:64]
            out[first + full_taps[1]] = full[:, 64:128]
            half = fin[g, 9 + n // 2].astype(F32) * root
            out[first + half_tap] = half[:, 0:64] if n % 2 == 0 else half[:, 64:128]
    loss = fin[0, 13].astype(F32)
    loss = loss[0:16] + loss[16:32] + loss[32:48]
    score_ref[0, 0] = jnp.sum(jnp.where(jnp.logical_and(lane((16, 128)) == 64, lax.broadcasted_iota(jnp.int32, (16, 128), 0) == 0), loss, 0.0)) * (1.0 / 262144.0)


def shards(sources, generator_weight, critic_kernel_weight, readout, load_weight):
    vmem = pl.BlockSpec(memory_space=pltpu.VMEM)
    smem = pl.BlockSpec(memory_space=pltpu.SMEM)
    dma = pltpu.SemaphoreType.DMA
    hbm = pl.BlockSpec(memory_space=pl.ANY)
    source_gradient, taps = pl.pallas_call(
        kernel,
        out_shape=(
            jax.ShapeDtypeStruct((8, 64, 128), F32),
            jax.ShapeDtypeStruct((2, TILES, 64, 128), BF),
        ),
        in_specs=[hbm, hbm, hbm, hbm, smem],
        out_specs=(vmem, vmem),
        scratch_shapes=[
            pltpu.VMEM((64, 8, 128), BF),
            pltpu.VMEM((27, 64, 64), BF),
            pltpu.VMEM((27, 64, 64), BF),
            pltpu.VMEM((1, 64), F32),
            dma((4,)),
            pltpu.VMEM((2, 256, LANES), F32),
            pltpu.VMEM((64, 8, 128), F32),
            pltpu.VMEM((3, 10, 64, 128), BF),
            pltpu.VMEM((3, 10, 64, 128), BF),
            pltpu.VMEM((3, 256, 256), BF),
            pltpu.VMEM((3, 256, 256), BF),
            pltpu.VMEM((3, 256, 256), BF),
            pltpu.VMEM((3, 256, 256), BF),
            pltpu.VMEM((3, 256, LANES), BF),
            pltpu.VMEM((3, 256, LANES), BF),
            pltpu.VMEM((3, 256, LANES), BF),
            pltpu.VMEM((3, 256, LANES), F32),
            pltpu.VMEM((3, 256, LANES), BF),
            pltpu.VMEM((256, LANES), F32),
            pltpu.VMEM((64, 128), F32),
            pltpu.VMEM((1, 128), F32),
            pltpu.VMEM((2, TILES, 64, 128), F32),
            pltpu.VMEM((TILES, 64, 128), F32),
            pltpu.VMEM((TILES, 64, 128), BF),
            pltpu.VMEM((16, 64, 128), BF),
            pltpu.VMEM((8, 64, 128), BF),
            dma((16,)), dma((16,)), dma((16,)), dma((16,)), dma((2,)),
            dma((TILES,)), dma((16,)), dma((8,)), dma((8,)),
            dma((16,)), dma((TILES,)), dma((TILES,)), dma((TILES,)),
        ],
        compiler_params=pltpu.CompilerParams(
            collective_id=0, has_side_effects=True, vmem_limit_bytes=56 * 2**20
        ),
        cost_estimate=pl.CostEstimate(flops=3 * 10**9, bytes_accessed=4 * 10**6, transcendentals=2 * 10**6),
    )(
        sources.reshape(64, 8, 128),
        generator_weight.reshape(27, 64, 64),
        critic_kernel_weight.reshape(27, 64, 64),
        readout.reshape(1, 64),
        load_weight,
    )
    score, source_gradient, gen, crit = pl.pallas_call(
        unpack,
        out_shape=(
            jax.ShapeDtypeStruct((1, 1), F32),
            jax.ShapeDtypeStruct((64, 8, 128), F32),
            jax.ShapeDtypeStruct((27, 64, 64), F32),
            jax.ShapeDtypeStruct((27, 64, 64), F32),
        ),
        in_specs=[vmem, vmem],
        out_specs=(smem, vmem, vmem, vmem),
        compiler_params=pltpu.CompilerParams(vmem_limit_bytes=16 * 2**20),
    )(taps, source_gradient)
    return (
        score.reshape(()),
        source_gradient.reshape(1, 64, 1, 8, 128),
        gen.reshape(3, 3, 3, 64, 64),
        crit.reshape(3, 3, 3, 64, 64),
    )


def solution(mesh):
    placed = (P(None, None, "gx", "gy", None), P(), P(), P(), P("gx", "gy"))
    return jax.shard_map(
        shards,
        mesh=mesh,
        in_specs=placed,
        out_specs=(P(), P(None, None, "gx", "gy", None), P(), P()),
        check_vma=False,
    )
```

```python
import math

import jax
import jax.numpy as jnp
from jax import lax
from jax.experimental import pallas as pl
from jax.experimental.pallas import tpu as pltpu
from jax.sharding import PartitionSpec as P

MESH = pl.DeviceIdType.MESH
BF = jnp.bfloat16
F32 = jnp.float32
ROWS = 9
LANES = ROWS * 128
TILES = 14
TAP = {(0, 0): 1, (1, 0): 2, (1, 1): 0}
SIDES = [(1, 0), (-1, 0), (0, 1), (0, -1), (1, 1), (1, -1), (-1, 1), (-1, -1)]


def dot(a, b):
    return lax.dot_general(a, b, (((1,), (0,)), ((), ())), preferred_element_type=F32)


def dot_t(a, b):
    return lax.dot_general(a, b, (((1,), (1,)), ((), ())), preferred_element_type=F32)


def lane(shape):
    return lax.broadcasted_iota(jnp.int32, shape, len(shape) - 1)


def next_z(value):
    moved = pltpu.roll(value, 127, 1)
    return jnp.where(lane(value.shape) < 127, moved, 0.0)


def prev_z(value):
    moved = pltpu.roll(value, 1, 1)
    return jnp.where(lane(value.shape) > 0, moved, 0.0)


def at(row, count=1):
    return pl.ds(pl.multiple_of(row * 128, 128), count * 128)


def split_round(value):
    plain = value.astype(BF)
    loss = value[0:16] + value[16:32] + value[32:48]
    high = loss.astype(BF)
    rest = loss - high.astype(F32)
    middle = rest.astype(BF)
    low = (rest - middle.astype(F32)).astype(BF)
    parts = jnp.concatenate([high, middle, low, jnp.zeros_like(high)], 0).astype(F32)
    return jnp.where(lane(value.shape) >= 64, parts, plain.astype(F32)).astype(BF)


def kernel(
    src_hbm, wg_hbm, wc_hbm, ro_hbm, lw_ref,
    sg_ref, fin,
    src_ref, wg_ref, wc_ref, ro_ref, lsem, half_field, stage, sbuf, dbuf, wg, wgt, wc, wct, u, d, f, slope, dg, q, ro, lossv,
    part, core_rx, psend, plane_rx, z_rx,
    s_s, s_r, d_s, d_r, c_s, c_r, p_s, p_r, z_s, z_r, g_s, g_r, f_s, f_r,
):
    gx, gy = lax.axis_index("gx"), lax.axis_index("gy")
    z, y, x, core = gx // 4, gx % 4, gy // 2, gy % 2
    pme = x * 4 + y

    def plane_dev(p):
        return (z * 4 + p % 4, (p // 4) * 2 + core)

    def z_dev(t):
        return (t * 4 + y, gy)

    core_dev = (gx, x * 2 + (1 - core))

    def side_dev(side):
        return ((gx + side[0] + 32) % 32, (gy + side[1] + 8) % 8)

    def rcopy(src, dst, send, recv, dev):
        return pltpu.make_async_remote_copy(
            src_ref=src, dst_ref=dst, send_sem=send, recv_sem=recv, device_id=dev, device_id_type=MESH
        )

    def halo(buf, n, send, recv, half=0):
        dx, dy = SIDES[n]
        if dy == 0:
            here = there = pl.ds(1 + 4 * half, 4)
        else:
            here, there = pl.ds(8 if dy > 0 else 1, 1), pl.ds(0 if dy > 0 else 9, 1)
        n = n + 8 * half
        return rcopy(buf.at[1, here], buf.at[1 - dx, there], send.at[n], recv.at[n], side_dev((dx, dy)))

    loads = [
        pltpu.make_async_copy(a, b, lsem.at[n])
        for n, (a, b) in enumerate(((src_hbm, src_ref), (wg_hbm, wg_ref), (wc_hbm, wc_ref), (ro_hbm, ro_ref)))
    ]
    for load in loads:
        load.start()

    barrier = pltpu.get_barrier_semaphore()

    def greet(dev):
        pl.semaphore_signal(barrier, inc=1, device_id=dev, device_id_type=MESH)

    for side in SIDES:
        greet(side_dev(side))
    greet(core_dev)

    @pl.loop(1, 16)
    def _(t):
        greet(plane_dev((pme + t) % 16))

    @pl.loop(1, 8)
    def _(t):
        greet(z_dev((z + t) % 8))

    loads[0].wait()
    stage[...] = src_ref[...].astype(F32)
    for r in range(8):
        sbuf[1, r + 1] = stage[:, r, :].astype(BF)

    pl.semaphore_wait(barrier, 8 + 1 + 15 + 7)
    parts = [(n, 0) for n in (4, 5, 6, 7, 2, 3)] + [(0, 0), (1, 0), (0, 1), (1, 1)]
    for n, half in parts:
        halo(sbuf, n, s_s, s_r, half).start()
    for load in loads[1:]:
        load.wait()

    zero = jnp.zeros((64, 64), F32)
    for s in range(3):
        for ay in range(2):
            for az in range(2):
                rows = pl.ds((ay * 2 + az) * 64, 64)
                for by in range(2):
                    pair = []
                    for bz in range(2):
                        ok = (by, ay) in TAP and (bz, az) in TAP
                        pair.append(wg_ref[s * 9 + TAP[by, ay] * 3 + TAP[bz, az]].astype(F32) if ok else zero)
                    wg[s, rows, pl.ds(by * 128, 128)] = jnp.concatenate(pair, 1).astype(BF)
                    pair = []
                    for bz in range(2):
                        ok = (ay, by) in TAP and (az, bz) in TAP
                        pair.append(wc_ref[s * 9 + TAP[ay, by] * 3 + TAP[az, bz]].astype(F32) if ok else zero)
                    wc[s, rows, pl.ds(by * 128, 128)] = jnp.concatenate(pair, 1).astype(BF)
        wgt[s] = wg[s].astype(F32).T.astype(BF)
        wct[s] = wc[s].astype(F32).T.astype(BF)
    ro[...] = jnp.broadcast_to(ro_ref[...], (128, 64)).T

    def spread(buf, out, xs, r, keep=None):
        value = buf[xs, r].astype(F32)
        if keep is not None:
            value = jnp.where(keep, value, 0.0)
        return value.astype(BF), next_z(value).astype(BF)

    def put_here(out, xs, r, pair):
        out[xs, 0:64, at(r)] = pair[0]
        out[xs, 64:128, at(r)] = pair[1]

    def put_below(out, xs, r, pair):
        out[xs, 128:192, at(r - 1)] = pair[0]
        out[xs, 192:256, at(r - 1)] = pair[1]

    def clear(out, xs):
        nothing = jnp.zeros((128, 128), BF)
        out[xs, 0:128, at(0)] = nothing
        out[xs, 128:256, at(8)] = nothing

    def own_rows(buf, out, xs, keep=None, first=1, last=8):
        @pl.loop(first, last + 1, unroll=4)
        def _(r):
            pair = spread(buf, out, xs, r, keep)
            put_here(out, xs, r, pair)
            put_below(out, xs, r, pair)

    def arrive(buf, out, send, recv):
        for half in range(2):
            for n, xs, keep in ((0, 0, None), (1, 2, gx < 31)):
                halo(buf, n, send, recv, half).wait_recv()
                own_rows(buf, out, xs, keep, 1 + 4 * half, 4 + 4 * half)
        for n in range(2, 8):
            halo(buf, n, send, recv).wait_recv()
        edge_rows(buf, out, 1)
        edge_rows(buf, out, 0)
        edge_rows(buf, out, 2, gx < 31)

    def edge_rows(buf, out, xs, keep=True):
        put_here(out, xs, 0, spread(buf, out, xs, 0, keep))
        put_below(out, xs, 9, spread(buf, out, xs, 9, jnp.logical_and(keep, gy < 7)))

    for xs in range(3):
        clear(u, xs)
        clear(d, xs)
    own_rows(sbuf, u, 1)

    def fire(s, v, c):
        t = jnp.tanh(0.5 * v)
        f[s, :, c] = (jnp.maximum(v, 0.2 * v) - 0.8 * jnp.log(1.0 + jnp.abs(t))).astype(BF)
        slope[s, :, c] = 0.6 + 0.4 * t

    def fire_low(s, v):
        t = jnp.tanh(0.5 * v)
        f[s, 128:256, 0:128] = (jnp.maximum(v, 0.2 * v) - 0.8 * jnp.log(1.0 + jnp.abs(t))).astype(BF)
        slope[s, 128:256, 0:128] = 0.6 + 0.4 * t

    def up_mid(weights, field, c):
        mid = field[1, :, c]
        return dot(weights[0], mid), dot(weights[1], mid), dot(weights[2], mid)

    def up_rest(weights, field, c):
        return dot(weights[2], field[0, :, c]), dot(weights[0], field[2, :, c])

    def up_low(weights, field):
        below, mid, above = field[0, :, 0:128], field[1, :, 0:128], field[2, :, 0:128]
        w0, w1, w2 = (weights[k, 128:256, :] for k in range(3))
        return dot(w2, below) + dot(w0, mid), dot(w1, mid), dot(w2, mid) + dot(w0, above)

    @pl.loop(0, 3)
    def _(j):
        c = at(j * 2 + 1, 2)
        low, mid, high = up_mid(wgt, u, c)
        fire(1, mid, c)
        slope[0, :, c] = low
        slope[2, :, c] = high

    for s in range(3):
        f[s, 0:128, 0:128] = jnp.zeros((128, 128), BF)
        dg[s, 0:128, 0:128] = jnp.zeros((128, 128), BF)

    arrive(sbuf, u, s_s, s_r)

    for s, v in enumerate(up_low(wgt, u)):
        fire_low(s, v)
    c = at(7, 2)
    low, mid, high = up_mid(wgt, u, c)
    fire(1, mid, c)
    slope[0, :, c] = low
    slope[2, :, c] = high

    @pl.loop(0, 4)
    def _(j):
        c = at(j * 2 + 1, 2)
        low, high = up_rest(wgt, u, c)
        fire(0, slope[0, :, c] + low, c)
        fire(2, slope[2, :, c] + high, c)

    @pl.when(gx == 0)
    def _():
        f[0] = jnp.zeros((256, LANES), BF)
        slope[0] = jnp.zeros((256, LANES), F32)

    @pl.when(gy == 0)
    def _():
        for s in range(3):
            f[s, 128:256, 0:128] = jnp.zeros((128, 128), BF)
            slope[s, 128:256, 0:128] = jnp.zeros((128, 128), F32)

    def down(weights, field, c):
        return dot(weights[0], field[0, :, c]) + dot(weights[1], field[1, :, c]) + dot(weights[2], field[2, :, c])

    def down_low(weights, field):
        terms = [dot(weights[k, 128:256, 128:256], field[k, 128:256, 0:128]) for k in range(3)]
        return terms[0] + terms[1] + terms[2]

    def gathered(r):
        near = q[0:64, at(r)] + q[128:192, at(r - 1)]
        far = q[64:128, at(r)] + q[192:256, at(r - 1)]
        return near + prev_z(far)

    q[128:256, 0:128] = down_low(wct, f)
    lossv[...] = jnp.zeros((1, 128), F32)

    def judge(r):
        v = gathered(r)
        t = jnp.tanh(0.5 * v)
        act = jnp.maximum(v, 0.2 * v) - 0.8 * jnp.log(1.0 + jnp.abs(t))
        logits = jnp.sum(act * ro[...], 0, keepdims=True)
        weight = lw_ref[0, r - 1].astype(F32)
        e = jnp.exp(-jnp.abs(logits))
        lossv[...] += weight * (jnp.maximum(-logits, 0.0) + jnp.log1p(e))
        d_logit = -weight * jnp.where(logits >= 0, e, 1.0) / (1.0 + e)
        dbuf[1, r] = (d_logit * ro[...] * (0.6 + 0.4 * t)).astype(BF)

    for half in range(2):
        @pl.loop(2 * half, 2 * half + 2)
        def _(j):
            c = at(j * 2 + 1, 2)
            q[:, c] = down(wct, f, c)
            judge(2 * j + 1)
            judge(2 * j + 2)

        for n in (5, 7, 3) if half == 0 else (4, 6, 2):
            halo(dbuf, n, d_s, d_r).start()
        for n in (0, 1):
            halo(dbuf, n, d_s, d_r, half).start()
    own_rows(dbuf, d, 1)

    @pl.loop(0, 3)
    def _(j):
        c = at(j * 2 + 1, 2)
        low, mid, high = up_mid(wc, d, c)
        dg[1, :, c] = (mid * slope[1, :, c]).astype(BF)
        half_field[0, :, c] = low
        half_field[1, :, c] = high

    def pair(g, k):
        lo, count = ((0, 3), (3, 3), (6, 3), (9, 5))[k]
        here = pl.ds(lo, count)
        return rcopy(part.at[g, here], core_rx.at[here], c_s.at[k], c_r.at[k], core_dev)

    def give(g, ks):
        @pl.when(core == 1 - g)
        def _():
            for k in ks:
                pair(g, k).start()

    def loss_tile(t):
        return jnp.logical_and(core == 0, t == 13)

    def to_owner(dst, src):
        return rcopy(psend.at[dst], plane_rx.at[src], p_s.at[dst], p_r.at[src], plane_dev(dst))

    def begin_sum(g):
        @pl.when(core == g)
        def _():
            for k in range(4):
                pair(g, k).wait_recv()

            @pl.loop(1, 17)
            def _(i):
                t = (pme + i) % 16

                @pl.when(t < TILES)
                def _():
                    total = part[g, t] + core_rx[t]
                    psend[t] = total.astype(BF)
                    if g == 0:
                        @pl.when(t == 13)
                        def _():
                            psend[t] = split_round(total)

                    @pl.when(t != pme)
                    def _():
                        to_owner(t, pme).start()

    def pack(g, s, full, halves):
        for j in range(3):
            n = s * 3 + j
            part[g, n] = full[j]
            left = lane((64, 128)) < 64
            half = halves[j]
            if (g == 0) == (n % 2 == 1):
                half = pltpu.roll(half, 64, 1)
            if n % 2 == 0:
                part[g, 9 + n // 2] = jnp.where(left, half, 0.0)
            else:
                part[g, 9 + n // 2] = jnp.where(left, part[g, 9 + n // 2], half)

    for s in range(3):
        q[:, 0:256] = dot_t(f[s], d[1])
        pairs = [(0, 0), (1, 0), (1, 1)]
        pack(
            0, s,
            [q[(p * 2 + 1) * 64:(p * 2 + 2) * 64, e * 128:e * 128 + 128] for p, e in pairs],
            [q[p * 128:p * 128 + 64, e * 128:e * 128 + 128] for p, e in pairs],
        )
        give(0, [s])
    loss = jnp.broadcast_to(jnp.sum(lossv[...], 1, keepdims=True), (16, 128))
    put = lane((16, 128)) >= 64
    part[0, 13, 0:16, :] = jnp.where(put, loss, part[0, 13, 0:16, :])
    give(0, [3])

    arrive(dbuf, d, d_s, d_r)
    begin_sum(0)

    for s, v in enumerate(up_low(wc, d)):
        dg[s, 128:256, 0:128] = (v * slope[s, 128:256, 0:128]).astype(BF)
    c = at(7, 2)
    low, mid, high = up_mid(wc, d, c)
    dg[1, :, c] = (mid * slope[1, :, c]).astype(BF)
    half_field[0, :, c] = low
    half_field[1, :, c] = high

    @pl.loop(0, 4)
    def _(j):
        c = at(j * 2 + 1, 2)
        low, high = up_rest(wc, d, c)
        dg[0, :, c] = ((half_field[0, :, c] + low) * slope[0, :, c]).astype(BF)
        dg[2, :, c] = ((half_field[1, :, c] + high) * slope[2, :, c]).astype(BF)

    clear(u, 1)
    for s in range(3):
        q[:, 0:256] = dot_t(u[1], dg[s])
        pairs = [(0, 0), (0, 1), (1, 1)]
        pack(
            1, s,
            [q[e * 128:e * 128 + 64, p * 128:p * 128 + 128] for e, p in pairs],
            [q[e * 128 + 64:e * 128 + 128, p * 128:p * 128 + 128] for e, p in pairs],
        )
        give(1, [s, 3] if s == 2 else [s])

    begin_sum(1)
    for n, half in parts:
        halo(sbuf, n, s_s, s_r, half).wait_send()
        halo(dbuf, n, d_s, d_r, half).wait_send()
    for k in range(4):
        pair(1 - core, k).wait_send()

    q[128:256, 0:128] = down_low(wg, dg)

    @pl.loop(0, 4)
    def _(j):
        c = at(j * 2 + 1, 2)
        q[:, c] = down(wg, dg, c)
        sg_ref[2 * j] = gathered(2 * j + 1)
        sg_ref[2 * j + 1] = gathered(2 * j + 2)

    def along_z(dst, src):
        return rcopy(z_rx.at[src], z_rx.at[src], z_s.at[dst], z_r.at[src], z_dev(dst))

    def to_plane(dst, src):
        return rcopy(fin.at[core, src], fin.at[core, src], g_s.at[dst], g_r.at[src], plane_dev(dst))

    def to_core(g, t):
        return rcopy(fin.at[g, t], fin.at[g, t], f_s.at[t], f_r.at[t], core_dev)

    @pl.when(pme < TILES)
    def _():
        plane_rx[pme] = psend[pme]

        @pl.loop(1, 16)
        def _(i):
            t = (pme + i) % 16
            to_owner(pme, t).wait_recv()

        total = plane_rx[0].astype(F32)
        for t in range(1, 16):
            total += plane_rx[t].astype(F32)
        z_rx[z] = total.astype(BF)

        @pl.when(loss_tile(pme))
        def _():
            z_rx[z] = split_round(total)

        @pl.loop(1, 8)
        def _(i):
            along_z((z + i) % 8, z).start()

        @pl.loop(1, 8)
        def _(i):
            t = (z + i) % 8
            along_z(t, t).wait_recv()

        total = z_rx[0].astype(F32)
        for t in range(1, 8):
            total += z_rx[t].astype(F32)
        fin[core, pme] = total.astype(BF)

        @pl.when(loss_tile(pme))
        def _():
            fin[core, pme] = split_round(total)


        @pl.loop(1, 16)
        def _(i):
            to_plane((pme + i) % 16, pme).start()

        to_core(core, pme).start()

    @pl.loop(1, 16)
    def _(i):
        t = (pme + 16 - i) % 16

        @pl.when(t < TILES)
        def _():
            to_plane(pme, t).wait_recv()
            to_core(core, t).start()

    @pl.loop(0, TILES)
    def _(t):
        to_core(1 - core, t).wait_recv()

    @pl.loop(1, 16)
    def _(i):
        t = (pme + i) % 16

        @pl.when(t < TILES)
        def _():
            to_owner(t, pme).wait_send()

    @pl.when(pme < TILES)
    def _():
        @pl.loop(1, 8)
        def _(i):
            along_z((z + i) % 8, z).wait_send()

        @pl.loop(1, 16)
        def _(i):
            to_plane((pme + i) % 16, pme).wait_send()

    @pl.loop(0, TILES)
    def _(t):
        to_core(core, t).wait_send()


def unpack(fin, sg_ref, score_ref, sg_out, gg_out, gc_out, sg_held, gg_held, gc_held, sem):
    copies = []

    def send(held, out):
        copies.append(pltpu.make_async_copy(held, out, sem.at[len(copies)]))
        copies[-1].start()

    root = 1.0 / math.sqrt(262144.0)
    for g, held, out, full_taps, half_tap in ((0, gc_held, gc_out, (2, 0), 1), (1, gg_held, gg_out, (1, 2), 0)):
        for n in range(9):
            first = (n // 3) * 9 + (1, 2, 0)[n % 3] * 3
            full = fin[g, n].astype(F32) * root
            held[first + full_taps[0]] = full[:, 0:64]
            held[first + full_taps[1]] = full[:, 64:128]
            half = fin[g, 9 + n // 2].astype(F32) * root
            held[first + half_tap] = half[:, 0:64] if n % 2 == 0 else half[:, 64:128]
            if n % 3 == 2:
                here = pl.ds((n // 3) * 9, 9)
                send(held.at[here], out.at[here])
    for r in range(8):
        sg_held[:, r, :] = sg_ref[r]
    send(sg_held, sg_out)
    loss = fin[0, 13].astype(F32)
    loss = loss[0:16] + loss[16:32] + loss[32:48]
    first = jnp.logical_and(lane((16, 128)) == 64, lax.broadcasted_iota(jnp.int32, (16, 128), 0) == 0)
    score_ref[0, 0] = jnp.sum(jnp.where(first, loss, 0.0)) * (1.0 / 262144.0)
    for copy in copies:
        copy.wait()


def shards(sources, generator_weight, critic_kernel_weight, readout, load_weight):
    vmem = pl.BlockSpec(memory_space=pltpu.VMEM)
    smem = pl.BlockSpec(memory_space=pltpu.SMEM)
    dma = pltpu.SemaphoreType.DMA
    hbm = pl.BlockSpec(memory_space=pl.ANY)
    source_gradient, taps = pl.pallas_call(
        kernel,
        out_shape=(
            jax.ShapeDtypeStruct((8, 64, 128), F32),
            jax.ShapeDtypeStruct((2, TILES, 64, 128), BF),
        ),
        in_specs=[hbm, hbm, hbm, hbm, smem],
        out_specs=(vmem, vmem),
        scratch_shapes=[
            pltpu.VMEM((64, 8, 128), BF),
            pltpu.VMEM((27, 64, 64), BF),
            pltpu.VMEM((27, 64, 64), BF),
            pltpu.VMEM((1, 64), F32),
            dma((4,)),
            pltpu.VMEM((2, 256, LANES), F32),
            pltpu.VMEM((64, 8, 128), F32),
            pltpu.VMEM((3, 10, 64, 128), BF),
            pltpu.VMEM((3, 10, 64, 128), BF),
            pltpu.VMEM((3, 256, 256), BF),
            pltpu.VMEM((3, 256, 256), BF),
            pltpu.VMEM((3, 256, 256), BF),
            pltpu.VMEM((3, 256, 256), BF),
            pltpu.VMEM((3, 256, LANES), BF),
            pltpu.VMEM((3, 256, LANES), BF),
            pltpu.VMEM((3, 256, LANES), BF),
            pltpu.VMEM((3, 256, LANES), F32),
            pltpu.VMEM((3, 256, LANES), BF),
            pltpu.VMEM((256, LANES), F32),
            pltpu.VMEM((64, 128), F32),
            pltpu.VMEM((1, 128), F32),
            pltpu.VMEM((2, TILES, 64, 128), F32),
            pltpu.VMEM((TILES, 64, 128), F32),
            pltpu.VMEM((TILES, 64, 128), BF),
            pltpu.VMEM((16, 64, 128), BF),
            pltpu.VMEM((8, 64, 128), BF),
            dma((16,)), dma((16,)), dma((16,)), dma((16,)), dma((4,)), dma((4,)),
            dma((TILES,)), dma((16,)), dma((8,)), dma((8,)),
            dma((16,)), dma((TILES,)), dma((TILES,)), dma((TILES,)),
        ],
        compiler_params=pltpu.CompilerParams(
            collective_id=0, has_side_effects=True, vmem_limit_bytes=56 * 2**20
        ),
        cost_estimate=pl.CostEstimate(flops=3 * 10**9, bytes_accessed=4 * 10**6, transcendentals=2 * 10**6),
    )(
        sources.reshape(64, 8, 128),
        generator_weight.reshape(27, 64, 64),
        critic_kernel_weight.reshape(27, 64, 64),
        readout.reshape(1, 64),
        load_weight,
    )
    score, source_gradient, gen, crit = pl.pallas_call(
        unpack,
        out_shape=(
            jax.ShapeDtypeStruct((1, 1), F32),
            jax.ShapeDtypeStruct((64, 8, 128), F32),
            jax.ShapeDtypeStruct((27, 64, 64), F32),
            jax.ShapeDtypeStruct((27, 64, 64), F32),
        ),
        in_specs=[vmem, vmem],
        out_specs=(smem, hbm, hbm, hbm),
        scratch_shapes=[
            pltpu.VMEM((64, 8, 128), F32),
            pltpu.VMEM((27, 64, 64), F32),
            pltpu.VMEM((27, 64, 64), F32),
            dma((7,)),
        ],
        compiler_params=pltpu.CompilerParams(vmem_limit_bytes=16 * 2**20),
    )(taps, source_gradient)
    return (
        score.reshape(()),
        source_gradient.reshape(1, 64, 1, 8, 128),
        gen.reshape(3, 3, 3, 64, 64),
        crit.reshape(3, 3, 3, 64, 64),
    )


def solution(mesh):
    placed = (P(None, None, "gx", "gy", None), P(), P(), P(), P("gx", "gy"))
    return jax.shard_map(
        shards,
        mesh=mesh,
        in_specs=placed,
        out_specs=(P(), P(None, None, "gx", "gy", None), P(), P()),
        check_vma=False,
    )
```

```python
import math

import jax
import jax.numpy as jnp
from jax import lax
from jax.experimental import pallas as pl
from jax.experimental.pallas import tpu as pltpu
from jax.sharding import PartitionSpec as P

MESH = pl.DeviceIdType.MESH
BF = jnp.bfloat16
F32 = jnp.float32
ROWS = 9
LANES = ROWS * 128
TILES = 14
TAP = {(0, 0): 1, (1, 0): 2, (1, 1): 0}
SIDES = [(1, 0), (-1, 0), (0, 1), (0, -1), (1, 1), (1, -1), (-1, 1), (-1, -1)]


def dot(a, b):
    return lax.dot_general(a, b, (((1,), (0,)), ((), ())), preferred_element_type=F32)


def dot_t(a, b):
    return lax.dot_general(a, b, (((1,), (1,)), ((), ())), preferred_element_type=F32)


def lane(shape):
    return lax.broadcasted_iota(jnp.int32, shape, len(shape) - 1)


def next_z(value):
    moved = pltpu.roll(value, 127, 1)
    return jnp.where(lane(value.shape) < 127, moved, 0.0)


def prev_z(value):
    moved = pltpu.roll(value, 1, 1)
    return jnp.where(lane(value.shape) > 0, moved, 0.0)


def at(row, count=1):
    return pl.ds(pl.multiple_of(row * 128, 128), count * 128)


def split_round(value):
    plain = value.astype(BF)
    loss = value[0:16] + value[16:32] + value[32:48]
    high = loss.astype(BF)
    rest = loss - high.astype(F32)
    middle = rest.astype(BF)
    low = (rest - middle.astype(F32)).astype(BF)
    parts = jnp.concatenate([high, middle, low, jnp.zeros_like(high)], 0).astype(F32)
    return jnp.where(lane(value.shape) >= 64, parts, plain.astype(F32)).astype(BF)


def kernel(
    src_hbm, wg_hbm, wc_hbm, ro_hbm, lw_ref,
    sg_ref, fin,
    src_ref, wg_ref, wc_ref, ro_ref, lsem, half_field, stage, sbuf, dbuf, wg, wgt, wc, wct, u, d, f, slope, dg, q, ro, lossv,
    part, core_rx, psend, plane_rx, z_rx,
    s_s, s_r, d_s, d_r, c_s, c_r, p_s, p_r, z_s, z_r, g_s, g_r, f_s, f_r,
):
    gx, gy = lax.axis_index("gx"), lax.axis_index("gy")
    z, y, x, core = gx // 4, gx % 4, gy // 2, gy % 2
    pme = x * 4 + y

    def plane_dev(p):
        return (z * 4 + p % 4, (p // 4) * 2 + core)

    def z_dev(t):
        return (t * 4 + y, gy)

    core_dev = (gx, x * 2 + (1 - core))

    def side_dev(side):
        return ((gx + side[0] + 32) % 32, (gy + side[1] + 8) % 8)

    def rcopy(src, dst, send, recv, dev):
        return pltpu.make_async_remote_copy(
            src_ref=src, dst_ref=dst, send_sem=send, recv_sem=recv, device_id=dev, device_id_type=MESH
        )

    def halo(buf, n, send, recv, half=0, pieces=2):
        dx, dy = SIDES[n]
        if dy == 0:
            count = 8 // pieces
            here = there = pl.ds(1 + count * half, count)
        else:
            here, there = pl.ds(8 if dy > 0 else 1, 1), pl.ds(0 if dy > 0 else 9, 1)
        n = n + 8 * half
        return rcopy(buf.at[1, here], buf.at[1 - dx, there], send.at[n], recv.at[n], side_dev((dx, dy)))

    loads = [
        pltpu.make_async_copy(a, b, lsem.at[n])
        for n, (a, b) in enumerate(((src_hbm, src_ref), (wg_hbm, wg_ref), (wc_hbm, wc_ref), (ro_hbm, ro_ref)))
    ]
    for load in loads:
        load.start()

    barrier = pltpu.get_barrier_semaphore()

    def greet(dev):
        pl.semaphore_signal(barrier, inc=1, device_id=dev, device_id_type=MESH)

    for side in SIDES:
        greet(side_dev(side))
    greet(core_dev)

    @pl.loop(1, 16)
    def _(t):
        greet(plane_dev((pme + t) % 16))

    @pl.loop(1, 8)
    def _(t):
        greet(z_dev((z + t) % 8))

    loads[0].wait()
    stage[...] = src_ref[...].astype(F32)
    for r in range(8):
        sbuf[1, r + 1] = stage[:, r, :].astype(BF)

    pl.semaphore_wait(barrier, 8 + 1 + 15 + 7)
    parts = [(n, 0) for n in (4, 5, 6, 7, 2, 3)] + [(n, h) for h in range(2) for n in (0, 1)]
    quarters = parts[:6] + [(n, h) for h in range(4) for n in (0, 1)]
    for n, half in parts:
        halo(sbuf, n, s_s, s_r, half).start()
    for load in loads[1:]:
        load.wait()

    zero = jnp.zeros((64, 64), F32)
    for s in range(3):
        for ay in range(2):
            for az in range(2):
                rows = pl.ds((ay * 2 + az) * 64, 64)
                for by in range(2):
                    pair = []
                    for bz in range(2):
                        ok = (by, ay) in TAP and (bz, az) in TAP
                        pair.append(wg_ref[s * 9 + TAP[by, ay] * 3 + TAP[bz, az]].astype(F32) if ok else zero)
                    wg[s, rows, pl.ds(by * 128, 128)] = jnp.concatenate(pair, 1).astype(BF)
                    pair = []
                    for bz in range(2):
                        ok = (ay, by) in TAP and (az, bz) in TAP
                        pair.append(wc_ref[s * 9 + TAP[ay, by] * 3 + TAP[az, bz]].astype(F32) if ok else zero)
                    wc[s, rows, pl.ds(by * 128, 128)] = jnp.concatenate(pair, 1).astype(BF)
        wgt[s] = wg[s].astype(F32).T.astype(BF)
        wct[s] = wc[s].astype(F32).T.astype(BF)
    ro[...] = jnp.broadcast_to(ro_ref[...], (128, 64)).T

    def spread(buf, out, xs, r, keep=None):
        value = buf[xs, r].astype(F32)
        if keep is not None:
            value = jnp.where(keep, value, 0.0)
        return value.astype(BF), next_z(value).astype(BF)

    def put_here(out, xs, r, pair):
        out[xs, 0:64, at(r)] = pair[0]
        out[xs, 64:128, at(r)] = pair[1]

    def put_below(out, xs, r, pair):
        out[xs, 128:192, at(r - 1)] = pair[0]
        out[xs, 192:256, at(r - 1)] = pair[1]

    def clear(out, xs):
        nothing = jnp.zeros((128, 128), BF)
        out[xs, 0:128, at(0)] = nothing
        out[xs, 128:256, at(8)] = nothing

    def own_rows(buf, out, xs, keep=None, first=1, last=8):
        @pl.loop(first, last + 1, unroll=min(4, last + 1 - first))
        def _(r):
            pair = spread(buf, out, xs, r, keep)
            put_here(out, xs, r, pair)
            put_below(out, xs, r, pair)

    def arrive(buf, out, send, recv, pieces):
        count = 8 // pieces
        for half in range(pieces):
            for n, xs, keep in ((0, 0, None), (1, 2, gx < 31)):
                halo(buf, n, send, recv, half, pieces).wait_recv()
                own_rows(buf, out, xs, keep, 1 + count * half, count + count * half)
        for n in range(2, 8):
            halo(buf, n, send, recv).wait_recv()
        edge_rows(buf, out, 1)
        edge_rows(buf, out, 0)
        edge_rows(buf, out, 2, gx < 31)

    def edge_rows(buf, out, xs, keep=True):
        put_here(out, xs, 0, spread(buf, out, xs, 0, keep))
        put_below(out, xs, 9, spread(buf, out, xs, 9, jnp.logical_and(keep, gy < 7)))

    for xs in range(3):
        clear(u, xs)
        clear(d, xs)
    own_rows(sbuf, u, 1)

    def fire(s, v, c):
        t = jnp.tanh(0.5 * v)
        f[s, :, c] = (jnp.maximum(v, 0.2 * v) - 0.8 * jnp.log(1.0 + jnp.abs(t))).astype(BF)
        slope[s, :, c] = 0.6 + 0.4 * t

    def fire_low(s, v):
        t = jnp.tanh(0.5 * v)
        f[s, 128:256, 0:128] = (jnp.maximum(v, 0.2 * v) - 0.8 * jnp.log(1.0 + jnp.abs(t))).astype(BF)
        slope[s, 128:256, 0:128] = 0.6 + 0.4 * t

    def up_mid(weights, field, c):
        mid = field[1, :, c]
        return dot(weights[0], mid), dot(weights[1], mid), dot(weights[2], mid)

    def up_rest(weights, field, c):
        return dot(weights[2], field[0, :, c]), dot(weights[0], field[2, :, c])

    def up_low(weights, field):
        below, mid, above = field[0, :, 0:128], field[1, :, 0:128], field[2, :, 0:128]
        w0, w1, w2 = (weights[k, 128:256, :] for k in range(3))
        return dot(w2, below) + dot(w0, mid), dot(w1, mid), dot(w2, mid) + dot(w0, above)

    @pl.loop(0, 3)
    def _(j):
        c = at(j * 2 + 1, 2)
        low, mid, high = up_mid(wgt, u, c)
        fire(1, mid, c)
        slope[0, :, c] = low
        slope[2, :, c] = high

    for s in range(3):
        f[s, 0:128, 0:128] = jnp.zeros((128, 128), BF)
        dg[s, 0:128, 0:128] = jnp.zeros((128, 128), BF)

    arrive(sbuf, u, s_s, s_r, 2)

    for s, v in enumerate(up_low(wgt, u)):
        fire_low(s, v)
    c = at(7, 2)
    low, mid, high = up_mid(wgt, u, c)
    fire(1, mid, c)
    slope[0, :, c] = low
    slope[2, :, c] = high

    @pl.loop(0, 4)
    def _(j):
        c = at(j * 2 + 1, 2)
        low, high = up_rest(wgt, u, c)
        fire(0, slope[0, :, c] + low, c)
        fire(2, slope[2, :, c] + high, c)

    @pl.when(gx == 0)
    def _():
        f[0] = jnp.zeros((256, LANES), BF)
        slope[0] = jnp.zeros((256, LANES), F32)

    @pl.when(gy == 0)
    def _():
        for s in range(3):
            f[s, 128:256, 0:128] = jnp.zeros((128, 128), BF)
            slope[s, 128:256, 0:128] = jnp.zeros((128, 128), F32)

    def down(weights, field, c):
        return dot(weights[0], field[0, :, c]) + dot(weights[1], field[1, :, c]) + dot(weights[2], field[2, :, c])

    def down_low(weights, field):
        terms = [dot(weights[k, 128:256, 128:256], field[k, 128:256, 0:128]) for k in range(3)]
        return terms[0] + terms[1] + terms[2]

    def gathered(r):
        near = q[0:64, at(r)] + q[128:192, at(r - 1)]
        far = q[64:128, at(r)] + q[192:256, at(r - 1)]
        return near + prev_z(far)

    q[128:256, 0:128] = down_low(wct, f)
    lossv[...] = jnp.zeros((1, 256), F32)

    def judge(r):
        near = q[0:64, at(r, 2)] + q[128:192, at(r - 1, 2)]
        far = q[64:128, at(r, 2)] + q[192:256, at(r - 1, 2)]
        v = near + jnp.where(lane((64, 256)) % 128 > 0, pltpu.roll(far, 1, 1), 0.0)
        t = jnp.tanh(0.5 * v)
        act = jnp.maximum(v, 0.2 * v) - 0.8 * jnp.log(1.0 + jnp.abs(t))
        read = jnp.concatenate([ro[...], ro[...]], 1)
        logits = jnp.sum(act * read, 0, keepdims=True)
        weight = jnp.where(lane((1, 256)) < 128, lw_ref[0, r - 1].astype(F32), lw_ref[0, r].astype(F32))
        e = jnp.exp(-jnp.abs(logits))
        lossv[...] += weight * (jnp.maximum(-logits, 0.0) + jnp.log1p(e))
        d_logit = -weight * jnp.where(logits >= 0, e, 1.0) / (1.0 + e)
        rows = (d_logit * read * (0.6 + 0.4 * t)).astype(BF)
        dbuf[1, r] = rows[:, 0:128]
        dbuf[1, r + 1] = rows[:, 128:256]

    for j in range(4):
        c = at(j * 2 + 1, 2)
        q[:, c] = down(wct, f, c)
        judge(2 * j + 1)
        for n in {0: (5, 7, 3), 3: (4, 6, 2)}.get(j, ()):
            halo(dbuf, n, d_s, d_r).start()
        for n in (0, 1):
            halo(dbuf, n, d_s, d_r, j, 4).start()
    own_rows(dbuf, d, 1)

    @pl.loop(0, 3)
    def _(j):
        c = at(j * 2 + 1, 2)
        low, mid, high = up_mid(wc, d, c)
        dg[1, :, c] = (mid * slope[1, :, c]).astype(BF)
        half_field[0, :, c] = low
        half_field[1, :, c] = high

    def pair(g, k):
        lo, count = ((0, 3), (3, 3), (6, 3), (9, 5))[k]
        here = pl.ds(lo, count)
        return rcopy(part.at[g, here], core_rx.at[here], c_s.at[k], c_r.at[k], core_dev)

    def give(g, ks):
        @pl.when(core == 1 - g)
        def _():
            for k in ks:
                pair(g, k).start()

    def loss_tile(t):
        return jnp.logical_and(core == 0, t == 13)

    def to_owner(dst, src):
        return rcopy(psend.at[dst], plane_rx.at[src], p_s.at[dst], p_r.at[src], plane_dev(dst))

    def begin_sum(g):
        @pl.when(core == g)
        def _():
            for k in range(4):
                pair(g, k).wait_recv()

            @pl.loop(1, 17)
            def _(i):
                t = (pme + i) % 16

                @pl.when(t < TILES)
                def _():
                    total = part[g, t] + core_rx[t]
                    psend[t] = total.astype(BF)
                    if g == 0:
                        @pl.when(t == 13)
                        def _():
                            psend[t] = split_round(total)

                    @pl.when(t != pme)
                    def _():
                        to_owner(t, pme).start()

    def pack(g, s, full, halves):
        for j in range(3):
            n = s * 3 + j
            part[g, n] = full[j]
            left = lane((64, 128)) < 64
            half = halves[j]
            if (g == 0) == (n % 2 == 1):
                half = pltpu.roll(half, 64, 1)
            if n % 2 == 0:
                part[g, 9 + n // 2] = jnp.where(left, half, 0.0)
            else:
                part[g, 9 + n // 2] = jnp.where(left, part[g, 9 + n // 2], half)

    for s in range(3):
        q[:, 0:256] = dot_t(f[s], d[1])
        pairs = [(0, 0), (1, 0), (1, 1)]
        pack(
            0, s,
            [q[(p * 2 + 1) * 64:(p * 2 + 2) * 64, e * 128:e * 128 + 128] for p, e in pairs],
            [q[p * 128:p * 128 + 64, e * 128:e * 128 + 128] for p, e in pairs],
        )
        give(0, [s])
    loss = jnp.broadcast_to(jnp.sum(lossv[...], 1, keepdims=True), (16, 128))
    put = lane((16, 128)) >= 64
    part[0, 13, 0:16, :] = jnp.where(put, loss, part[0, 13, 0:16, :])
    give(0, [3])

    arrive(dbuf, d, d_s, d_r, 4)
    begin_sum(0)

    for s, v in enumerate(up_low(wc, d)):
        dg[s, 128:256, 0:128] = (v * slope[s, 128:256, 0:128]).astype(BF)
    c = at(7, 2)
    low, mid, high = up_mid(wc, d, c)
    dg[1, :, c] = (mid * slope[1, :, c]).astype(BF)
    half_field[0, :, c] = low
    half_field[1, :, c] = high

    @pl.loop(0, 4)
    def _(j):
        c = at(j * 2 + 1, 2)
        low, high = up_rest(wc, d, c)
        dg[0, :, c] = ((half_field[0, :, c] + low) * slope[0, :, c]).astype(BF)
        dg[2, :, c] = ((half_field[1, :, c] + high) * slope[2, :, c]).astype(BF)

    clear(u, 1)
    for s in range(3):
        q[:, 0:256] = dot_t(u[1], dg[s])
        pairs = [(0, 0), (0, 1), (1, 1)]
        pack(
            1, s,
            [q[e * 128:e * 128 + 64, p * 128:p * 128 + 128] for e, p in pairs],
            [q[e * 128 + 64:e * 128 + 128, p * 128:p * 128 + 128] for e, p in pairs],
        )
        give(1, [s, 3] if s == 2 else [s])

    begin_sum(1)
    for n, half in parts:
        halo(sbuf, n, s_s, s_r, half).wait_send()
    for n, half in quarters:
        halo(dbuf, n, d_s, d_r, half, 4).wait_send()
    for k in range(4):
        pair(1 - core, k).wait_send()

    q[128:256, 0:128] = down_low(wg, dg)

    @pl.loop(0, 4)
    def _(j):
        c = at(j * 2 + 1, 2)
        q[:, c] = down(wg, dg, c)
        sg_ref[2 * j] = gathered(2 * j + 1)
        sg_ref[2 * j + 1] = gathered(2 * j + 2)

    def along_z(dst, src):
        return rcopy(z_rx.at[src], z_rx.at[src], z_s.at[dst], z_r.at[src], z_dev(dst))

    def to_plane(dst, src):
        return rcopy(fin.at[core, src], fin.at[core, src], g_s.at[dst], g_r.at[src], plane_dev(dst))

    def to_core(g, t):
        return rcopy(fin.at[g, t], fin.at[g, t], f_s.at[t], f_r.at[t], core_dev)

    @pl.when(pme < TILES)
    def _():
        plane_rx[pme] = psend[pme]

        @pl.loop(1, 16)
        def _(i):
            t = (pme + i) % 16
            to_owner(pme, t).wait_recv()

        total = plane_rx[0].astype(F32)
        for t in range(1, 16):
            total += plane_rx[t].astype(F32)
        z_rx[z] = total.astype(BF)

        @pl.when(loss_tile(pme))
        def _():
            z_rx[z] = split_round(total)

        @pl.loop(1, 8)
        def _(i):
            along_z((z + i) % 8, z).start()

        @pl.loop(1, 8)
        def _(i):
            t = (z + i) % 8
            along_z(t, t).wait_recv()

        total = z_rx[0].astype(F32)
        for t in range(1, 8):
            total += z_rx[t].astype(F32)
        fin[core, pme] = total.astype(BF)

        @pl.when(loss_tile(pme))
        def _():
            fin[core, pme] = split_round(total)


        @pl.loop(1, 16)
        def _(i):
            to_plane((pme + i) % 16, pme).start()

        to_core(core, pme).start()

    @pl.loop(1, 16)
    def _(i):
        t = (pme + 16 - i) % 16

        @pl.when(t < TILES)
        def _():
            to_plane(pme, t).wait_recv()
            to_core(core, t).start()

    @pl.loop(0, TILES)
    def _(t):
        to_core(1 - core, t).wait_recv()

    @pl.loop(1, 16)
    def _(i):
        t = (pme + i) % 16

        @pl.when(t < TILES)
        def _():
            to_owner(t, pme).wait_send()

    @pl.when(pme < TILES)
    def _():
        @pl.loop(1, 8)
        def _(i):
            along_z((z + i) % 8, z).wait_send()

        @pl.loop(1, 16)
        def _(i):
            to_plane((pme + i) % 16, pme).wait_send()

    @pl.loop(0, TILES)
    def _(t):
        to_core(core, t).wait_send()


def unpack(fin, sg_ref, score_ref, sg_out, gg_out, gc_out, sg_held, gg_held, gc_held, sem):
    copies = []

    def send(held, out):
        copies.append(pltpu.make_async_copy(held, out, sem.at[len(copies)]))
        copies[-1].start()

    root = 1.0 / math.sqrt(262144.0)
    for g, held, out, full_taps, half_tap in ((0, gc_held, gc_out, (2, 0), 1), (1, gg_held, gg_out, (1, 2), 0)):
        for n in range(9):
            first = (n // 3) * 9 + (1, 2, 0)[n % 3] * 3
            full = fin[g, n].astype(F32) * root
            held[first + full_taps[0]] = full[:, 0:64]
            held[first + full_taps[1]] = full[:, 64:128]
            half = fin[g, 9 + n // 2].astype(F32) * root
            held[first + half_tap] = half[:, 0:64] if n % 2 == 0 else half[:, 64:128]
            if n % 3 == 2:
                here = pl.ds((n // 3) * 9, 9)
                send(held.at[here], out.at[here])
    for r in range(8):
        sg_held[:, r, :] = sg_ref[r]
    send(sg_held, sg_out)
    loss = fin[0, 13].astype(F32)
    loss = loss[0:16] + loss[16:32] + loss[32:48]
    first = jnp.logical_and(lane((16, 128)) == 64, lax.broadcasted_iota(jnp.int32, (16, 128), 0) == 0)
    score_ref[0, 0] = jnp.sum(jnp.where(first, loss, 0.0)) * (1.0 / 262144.0)
    for copy in copies:
        copy.wait()


def shards(sources, generator_weight, critic_kernel_weight, readout, load_weight):
    vmem = pl.BlockSpec(memory_space=pltpu.VMEM)
    smem = pl.BlockSpec(memory_space=pltpu.SMEM)
    dma = pltpu.SemaphoreType.DMA
    hbm = pl.BlockSpec(memory_space=pltpu.HBM)
    source_gradient, taps = pl.pallas_call(
        kernel,
        out_shape=(
            pltpu.VMEM((8, 64, 128), F32),
            pltpu.VMEM((2, TILES, 64, 128), BF),
        ),
        in_specs=[hbm, hbm, hbm, hbm, smem],
        out_specs=(vmem, vmem),
        scratch_shapes=[
            pltpu.VMEM((64, 8, 128), BF),
            pltpu.VMEM((27, 64, 64), BF),
            pltpu.VMEM((27, 64, 64), BF),
            pltpu.VMEM((1, 64), F32),
            dma((4,)),
            pltpu.VMEM((2, 256, LANES), F32),
            pltpu.VMEM((64, 8, 128), F32),
            pltpu.VMEM((3, 10, 64, 128), BF),
            pltpu.VMEM((3, 10, 64, 128), BF),
            pltpu.VMEM((3, 256, 256), BF),
            pltpu.VMEM((3, 256, 256), BF),
            pltpu.VMEM((3, 256, 256), BF),
            pltpu.VMEM((3, 256, 256), BF),
            pltpu.VMEM((3, 256, LANES), BF),
            pltpu.VMEM((3, 256, LANES), BF),
            pltpu.VMEM((3, 256, LANES), BF),
            pltpu.VMEM((3, 256, LANES), F32),
            pltpu.VMEM((3, 256, LANES), BF),
            pltpu.VMEM((256, LANES), F32),
            pltpu.VMEM((64, 128), F32),
            pltpu.VMEM((1, 256), F32),
            pltpu.VMEM((2, TILES, 64, 128), F32),
            pltpu.VMEM((TILES, 64, 128), F32),
            pltpu.VMEM((TILES, 64, 128), BF),
            pltpu.VMEM((16, 64, 128), BF),
            pltpu.VMEM((8, 64, 128), BF),
            dma((16,)), dma((16,)), dma((32,)), dma((32,)), dma((4,)), dma((4,)),
            dma((TILES,)), dma((16,)), dma((8,)), dma((8,)),
            dma((16,)), dma((TILES,)), dma((TILES,)), dma((TILES,)),
        ],
        compiler_params=pltpu.CompilerParams(
            collective_id=0, has_side_effects=True, vmem_limit_bytes=56 * 2**20
        ),
        cost_estimate=pl.CostEstimate(flops=3 * 10**9, bytes_accessed=4 * 10**6, transcendentals=2 * 10**6),
    )(
        sources.reshape(64, 8, 128),
        generator_weight.reshape(27, 64, 64),
        critic_kernel_weight.reshape(27, 64, 64),
        readout.reshape(1, 64),
        load_weight,
    )
    score, source_gradient, gen, crit = pl.pallas_call(
        unpack,
        out_shape=(
            jax.ShapeDtypeStruct((1, 1), F32),
            jax.ShapeDtypeStruct((64, 8, 128), F32),
            jax.ShapeDtypeStruct((27, 64, 64), F32),
            jax.ShapeDtypeStruct((27, 64, 64), F32),
        ),
        in_specs=[vmem, vmem],
        out_specs=(smem, hbm, hbm, hbm),
        scratch_shapes=[
            pltpu.VMEM((64, 8, 128), F32),
            pltpu.VMEM((27, 64, 64), F32),
            pltpu.VMEM((27, 64, 64), F32),
            dma((7,)),
        ],
        compiler_params=pltpu.CompilerParams(vmem_limit_bytes=16 * 2**20),
    )(taps, source_gradient)
    return (
        score.reshape(()),
        source_gradient.reshape(1, 64, 1, 8, 128),
        gen.reshape(3, 3, 3, 64, 64),
        crit.reshape(3, 3, 3, 64, 64),
    )


def solution(mesh):
    placed = (P(None, None, "gx", "gy", None), P(), P(), P(), P("gx", "gy"))
    return jax.shard_map(
        shards,
        mesh=mesh,
        in_specs=placed,
        out_specs=(P(), P(None, None, "gx", "gy", None), P(), P()),
        check_vma=False,
    )
```

```python
import math

import jax
import jax.numpy as jnp
from jax import lax
from jax.experimental import pallas as pl
from jax.experimental.pallas import tpu as pltpu
from jax.sharding import PartitionSpec as P

MESH = pl.DeviceIdType.MESH
BF = jnp.bfloat16
F32 = jnp.float32
ROWS = 9
LANES = ROWS * 128
TILES = 14
TAP = {(0, 0): 1, (1, 0): 2, (1, 1): 0}
SIDES = [(1, 0), (-1, 0), (0, 1), (0, -1), (1, 1), (1, -1), (-1, 1), (-1, -1)]


def dot(a, b):
    return lax.dot_general(a, b, (((1,), (0,)), ((), ())), preferred_element_type=F32)


def dot_t(a, b):
    return lax.dot_general(a, b, (((1,), (1,)), ((), ())), preferred_element_type=F32)


def lane(shape):
    return lax.broadcasted_iota(jnp.int32, shape, len(shape) - 1)


def next_z(value):
    moved = pltpu.roll(value, 127, 1)
    return jnp.where(lane(value.shape) < 127, moved, 0.0)


def prev_z(value):
    moved = pltpu.roll(value, 1, 1)
    return jnp.where(lane(value.shape) > 0, moved, 0.0)


def at(row, count=1):
    return pl.ds(pl.multiple_of(row * 128, 128), count * 128)


def split_round(value):
    plain = value.astype(BF)
    loss = value[0:16] + value[16:32] + value[32:48]
    high = loss.astype(BF)
    rest = loss - high.astype(F32)
    middle = rest.astype(BF)
    low = (rest - middle.astype(F32)).astype(BF)
    parts = jnp.concatenate([high, middle, low, jnp.zeros_like(high)], 0).astype(F32)
    return jnp.where(lane(value.shape) >= 64, parts, plain.astype(F32)).astype(BF)


def kernel(
    src_hbm, wg_hbm, wc_hbm, ro_hbm, lw_ref,
    sg_ref, fin,
    src_ref, wg_ref, wc_ref, ro_ref, lsem, rounds, half_field, stage, sbuf, dbuf, wg, wgt, wc, wct, u, d, f, slope, dg, q, ro, lossv,
    part, core_rx, psend, plane_rx, z_rx,
    s_s, s_r, d_s, d_r, c_s, c_r, p_s, p_r, z_s, z_r, g_s, g_r, f_s, f_r,
):
    gx, gy = lax.axis_index("gx"), lax.axis_index("gy")
    z, y, x, core = gx // 4, gx % 4, gy // 2, gy % 2
    pme = x * 4 + y

    def plane_dev(p):
        return (z * 4 + p % 4, (p // 4) * 2 + core)

    def z_dev(t):
        return (t * 4 + y, gy)

    core_dev = (gx, x * 2 + (1 - core))

    def side_dev(side):
        return ((gx + side[0] + 32) % 32, (gy + side[1] + 8) % 8)

    def rcopy(src, dst, send, recv, dev):
        return pltpu.make_async_remote_copy(
            src_ref=src, dst_ref=dst, send_sem=send, recv_sem=recv, device_id=dev, device_id_type=MESH
        )

    def halo(buf, n, send, recv, quarter=0):
        dx, dy = SIDES[n]
        if dy == 0:
            here = there = pl.ds(1 + 2 * quarter, 2)
        else:
            here, there = pl.ds(8 if dy > 0 else 1, 1), pl.ds(0 if dy > 0 else 9, 1)
        n = n + 8 * quarter
        return rcopy(buf.at[1, here], buf.at[1 - dx, there], send.at[n], recv.at[n], side_dev((dx, dy)))

    loads = [
        pltpu.make_async_copy(a, b, lsem.at[n])
        for n, (a, b) in enumerate(((src_hbm, src_ref), (wg_hbm, wg_ref), (wc_hbm, wc_ref), (ro_hbm, ro_ref)))
    ]
    for load in loads:
        load.start()

    barrier = pltpu.get_barrier_semaphore()

    def greet(dev):
        pl.semaphore_signal(barrier, inc=1, device_id=dev, device_id_type=MESH)

    for side in SIDES:
        greet(side_dev(side))
    greet(core_dev)

    near = [
        (gx, ((x + 1) % 4) * 2 + core),
        (gx, ((x + 3) % 4) * 2 + core),
        (z * 4 + (y + 1) % 4, gy),
        (z * 4 + (y + 3) % 4, gy),
        (((z + 1) % 8) * 4 + y, gy),
        (((z + 7) % 8) * 4 + y, gy),
    ]
    for dev in near:
        greet(dev)

    def tell(k):
        for dev in near:
            pl.semaphore_signal(rounds.at[k], inc=1, device_id=dev, device_id_type=MESH)

    def hear(k):
        pl.semaphore_wait(rounds.at[k], 6)

    loads[0].wait()
    stage[...] = src_ref[...].astype(F32)
    for r in range(8):
        sbuf[1, r + 1] = stage[:, r, :].astype(BF)

    pl.semaphore_wait(barrier, 8 + 1 + 6)
    parts = [(n, 0) for n in (4, 5, 6, 7, 2, 3)] + [(n, quarter) for quarter in range(4) for n in (0, 1)]
    for n, quarter in parts:
        halo(sbuf, n, s_s, s_r, quarter).start()
    tell(0)
    for load in loads[1:]:
        load.wait()

    zero = jnp.zeros((64, 64), F32)
    for s in range(3):
        for ay in range(2):
            for az in range(2):
                rows = pl.ds((ay * 2 + az) * 64, 64)
                for by in range(2):
                    pair = []
                    for bz in range(2):
                        ok = (by, ay) in TAP and (bz, az) in TAP
                        pair.append(wg_ref[s * 9 + TAP[by, ay] * 3 + TAP[bz, az]].astype(F32) if ok else zero)
                    wg[s, rows, pl.ds(by * 128, 128)] = jnp.concatenate(pair, 1).astype(BF)
                    pair = []
                    for bz in range(2):
                        ok = (ay, by) in TAP and (az, bz) in TAP
                        pair.append(wc_ref[s * 9 + TAP[ay, by] * 3 + TAP[az, bz]].astype(F32) if ok else zero)
                    wc[s, rows, pl.ds(by * 128, 128)] = jnp.concatenate(pair, 1).astype(BF)
        wgt[s] = wg[s].astype(F32).T.astype(BF)
        wct[s] = wc[s].astype(F32).T.astype(BF)
    ro[...] = jnp.broadcast_to(ro_ref[...], (128, 64)).T

    def spread(buf, out, xs, r, keep=None):
        value = buf[xs, r].astype(F32)
        if keep is not None:
            value = jnp.where(keep, value, 0.0)
        return value.astype(BF), next_z(value).astype(BF)

    def put_here(out, xs, r, pair):
        out[xs, 0:64, at(r)] = pair[0]
        out[xs, 64:128, at(r)] = pair[1]

    def put_below(out, xs, r, pair):
        out[xs, 128:192, at(r - 1)] = pair[0]
        out[xs, 192:256, at(r - 1)] = pair[1]

    def clear(out, xs):
        nothing = jnp.zeros((128, 128), BF)
        out[xs, 0:128, at(0)] = nothing
        out[xs, 128:256, at(8)] = nothing

    def own_rows(buf, out, xs, keep=None, first=1, last=8):
        @pl.loop(first, last + 1, unroll=min(4, last + 1 - first))
        def _(r):
            pair = spread(buf, out, xs, r, keep)
            put_here(out, xs, r, pair)
            put_below(out, xs, r, pair)

    def arrive(buf, out, send, recv, rest):
        for quarter in range(4):
            for n, xs, keep in ((0, 0, None), (1, 2, gx < 31)):
                halo(buf, n, send, recv, quarter).wait_recv()
                own_rows(buf, out, xs, keep, 2 * quarter + 1, 2 * quarter + 2)
            if quarter:
                rest(quarter - 1)
        for n in range(2, 8):
            halo(buf, n, send, recv).wait_recv()
        edge_rows(buf, out, 1)
        edge_rows(buf, out, 0)
        edge_rows(buf, out, 2, gx < 31)

    def edge_rows(buf, out, xs, keep=True):
        put_here(out, xs, 0, spread(buf, out, xs, 0, keep))
        put_below(out, xs, 9, spread(buf, out, xs, 9, jnp.logical_and(keep, gy < 7)))

    for xs in range(3):
        clear(u, xs)
        clear(d, xs)
    own_rows(sbuf, u, 1)

    def fire(s, v, c):
        t = jnp.tanh(0.5 * v)
        f[s, :, c] = (jnp.maximum(v, 0.2 * v) - 0.8 * jnp.log(1.0 + jnp.abs(t))).astype(BF)
        slope[s, :, c] = 0.6 + 0.4 * t

    def fire_low(s, v):
        t = jnp.tanh(0.5 * v)
        f[s, 128:256, 0:128] = (jnp.maximum(v, 0.2 * v) - 0.8 * jnp.log(1.0 + jnp.abs(t))).astype(BF)
        slope[s, 128:256, 0:128] = 0.6 + 0.4 * t

    def up_mid(weights, field, c):
        mid = field[1, :, c]
        return dot(weights[0], mid), dot(weights[1], mid), dot(weights[2], mid)

    def up_rest(weights, field, c):
        return dot(weights[2], field[0, :, c]), dot(weights[0], field[2, :, c])

    def up_low(weights, field):
        below, mid, above = field[0, :, 0:128], field[1, :, 0:128], field[2, :, 0:128]
        w0, w1, w2 = (weights[k, 128:256, :] for k in range(3))
        return dot(w2, below) + dot(w0, mid), dot(w1, mid), dot(w2, mid) + dot(w0, above)

    @pl.loop(0, 3)
    def _(j):
        c = at(j * 2 + 1, 2)
        low, mid, high = up_mid(wgt, u, c)
        fire(1, mid, c)
        slope[0, :, c] = low
        slope[2, :, c] = high

    for s in range(3):
        f[s, 0:128, 0:128] = jnp.zeros((128, 128), BF)
        dg[s, 0:128, 0:128] = jnp.zeros((128, 128), BF)

    def fire_rest(j):
        c = at(j * 2 + 1, 2)
        low, high = up_rest(wgt, u, c)
        fire(0, slope[0, :, c] + low, c)
        fire(2, slope[2, :, c] + high, c)

    arrive(sbuf, u, s_s, s_r, fire_rest)
    hear(0)
    tell(1)

    for s, v in enumerate(up_low(wgt, u)):
        fire_low(s, v)
    c = at(7, 2)
    low, mid, high = up_mid(wgt, u, c)
    fire(1, mid, c)
    slope[0, :, c] = low
    slope[2, :, c] = high

    fire_rest(3)

    @pl.when(gx == 0)
    def _():
        f[0] = jnp.zeros((256, LANES), BF)
        slope[0] = jnp.zeros((256, LANES), F32)

    @pl.when(gy == 0)
    def _():
        for s in range(3):
            f[s, 128:256, 0:128] = jnp.zeros((128, 128), BF)
            slope[s, 128:256, 0:128] = jnp.zeros((128, 128), F32)

    def down(weights, field, c):
        return dot(weights[0], field[0, :, c]) + dot(weights[1], field[1, :, c]) + dot(weights[2], field[2, :, c])

    def down_low(weights, field):
        terms = [dot(weights[k, 128:256, 128:256], field[k, 128:256, 0:128]) for k in range(3)]
        return terms[0] + terms[1] + terms[2]

    def gathered(r):
        near = q[0:64, at(r)] + q[128:192, at(r - 1)]
        far = q[64:128, at(r)] + q[192:256, at(r - 1)]
        return near + prev_z(far)

    q[128:256, 0:128] = down_low(wct, f)
    lossv[...] = jnp.zeros((1, 256), F32)

    def judge(r):
        near = q[0:64, at(r, 2)] + q[128:192, at(r - 1, 2)]
        far = q[64:128, at(r, 2)] + q[192:256, at(r - 1, 2)]
        v = near + jnp.where(lane((64, 256)) % 128 > 0, pltpu.roll(far, 1, 1), 0.0)
        t = jnp.tanh(0.5 * v)
        act = jnp.maximum(v, 0.2 * v) - 0.8 * jnp.log(1.0 + jnp.abs(t))
        read = jnp.concatenate([ro[...], ro[...]], 1)
        logits = jnp.sum(act * read, 0, keepdims=True)
        weight = jnp.where(lane((1, 256)) < 128, lw_ref[0, r - 1].astype(F32), lw_ref[0, r].astype(F32))
        e = jnp.exp(-jnp.abs(logits))
        lossv[...] += weight * (jnp.maximum(-logits, 0.0) + jnp.log1p(e))
        d_logit = -weight * jnp.where(logits >= 0, e, 1.0) / (1.0 + e)
        rows = (d_logit * read * (0.6 + 0.4 * t)).astype(BF)
        dbuf[1, r] = rows[:, 0:128]
        dbuf[1, r + 1] = rows[:, 128:256]

    for j in range(4):
        c = at(j * 2 + 1, 2)
        q[:, c] = down(wct, f, c)
        judge(2 * j + 1)
        for n in {0: (5, 7, 3), 3: (4, 6, 2)}.get(j, ()):
            halo(dbuf, n, d_s, d_r).start()
        for n in (0, 1):
            halo(dbuf, n, d_s, d_r, j).start()
    hear(1)
    tell(2)
    own_rows(dbuf, d, 1)

    @pl.loop(0, 3)
    def _(j):
        c = at(j * 2 + 1, 2)
        low, mid, high = up_mid(wc, d, c)
        dg[1, :, c] = (mid * slope[1, :, c]).astype(BF)
        half_field[0, :, c] = low
        half_field[1, :, c] = high

    def pair(g, k):
        lo, count = ((0, 3), (3, 3), (6, 3), (9, 5))[k]
        here = pl.ds(lo, count)
        return rcopy(part.at[g, here], core_rx.at[here], c_s.at[k], c_r.at[k], core_dev)

    def give(g, ks):
        @pl.when(core == 1 - g)
        def _():
            for k in ks:
                pair(g, k).start()

    def loss_tile(t):
        return jnp.logical_and(core == 0, t == 13)

    def to_owner(dst, src):
        return rcopy(psend.at[dst], plane_rx.at[src], p_s.at[dst], p_r.at[src], plane_dev(dst))

    def begin_sum(g):
        @pl.when(core == g)
        def _():
            for k in range(4):
                pair(g, k).wait_recv()

            @pl.loop(1, 17)
            def _(i):
                t = (pme + i) % 16

                @pl.when(t < TILES)
                def _():
                    total = part[g, t] + core_rx[t]
                    psend[t] = total.astype(BF)
                    if g == 0:
                        @pl.when(t == 13)
                        def _():
                            psend[t] = split_round(total)

                    @pl.when(t != pme)
                    def _():
                        to_owner(t, pme).start()

    def pack(g, s, full, halves):
        for j in range(3):
            n = s * 3 + j
            part[g, n] = full[j]
            left = lane((64, 128)) < 64
            half = halves[j]
            if (g == 0) == (n % 2 == 1):
                half = pltpu.roll(half, 64, 1)
            if n % 2 == 0:
                part[g, 9 + n // 2] = jnp.where(left, half, 0.0)
            else:
                part[g, 9 + n // 2] = jnp.where(left, part[g, 9 + n // 2], half)

    for s in range(3):
        q[:, 0:256] = dot_t(f[s], d[1])
        pairs = [(0, 0), (1, 0), (1, 1)]
        pack(
            0, s,
            [q[(p * 2 + 1) * 64:(p * 2 + 2) * 64, e * 128:e * 128 + 128] for p, e in pairs],
            [q[p * 128:p * 128 + 64, e * 128:e * 128 + 128] for p, e in pairs],
        )
        give(0, [s])
    loss = jnp.broadcast_to(jnp.sum(lossv[...], 1, keepdims=True), (16, 128))
    put = lane((16, 128)) >= 64
    part[0, 13, 0:16, :] = jnp.where(put, loss, part[0, 13, 0:16, :])
    give(0, [3])

    def back_rest(j):
        c = at(j * 2 + 1, 2)
        low, high = up_rest(wc, d, c)
        dg[0, :, c] = ((half_field[0, :, c] + low) * slope[0, :, c]).astype(BF)
        dg[2, :, c] = ((half_field[1, :, c] + high) * slope[2, :, c]).astype(BF)

    arrive(dbuf, d, d_s, d_r, back_rest)
    hear(2)
    begin_sum(0)

    for s, v in enumerate(up_low(wc, d)):
        dg[s, 128:256, 0:128] = (v * slope[s, 128:256, 0:128]).astype(BF)
    c = at(7, 2)
    low, mid, high = up_mid(wc, d, c)
    dg[1, :, c] = (mid * slope[1, :, c]).astype(BF)
    half_field[0, :, c] = low
    half_field[1, :, c] = high

    back_rest(3)

    clear(u, 1)
    for s in range(3):
        q[:, 0:256] = dot_t(u[1], dg[s])
        pairs = [(0, 0), (0, 1), (1, 1)]
        pack(
            1, s,
            [q[e * 128:e * 128 + 64, p * 128:p * 128 + 128] for e, p in pairs],
            [q[e * 128 + 64:e * 128 + 128, p * 128:p * 128 + 128] for e, p in pairs],
        )
        give(1, [s, 3] if s == 2 else [s])

    begin_sum(1)
    for n, quarter in parts:
        halo(sbuf, n, s_s, s_r, quarter).wait_send()
        halo(dbuf, n, d_s, d_r, quarter).wait_send()
    for k in range(4):
        pair(1 - core, k).wait_send()

    q[128:256, 0:128] = down_low(wg, dg)

    @pl.loop(0, 4)
    def _(j):
        c = at(j * 2 + 1, 2)
        q[:, c] = down(wg, dg, c)
        sg_ref[2 * j] = gathered(2 * j + 1)
        sg_ref[2 * j + 1] = gathered(2 * j + 2)

    def along_z(dst, src):
        return rcopy(z_rx.at[src], z_rx.at[src], z_s.at[dst], z_r.at[src], z_dev(dst))

    def to_plane(dst, src):
        return rcopy(fin.at[core, src], fin.at[core, src], g_s.at[dst], g_r.at[src], plane_dev(dst))

    def to_core(g, t):
        return rcopy(fin.at[g, t], fin.at[g, t], f_s.at[t], f_r.at[t], core_dev)

    @pl.when(pme < TILES)
    def _():
        plane_rx[pme] = psend[pme]

        @pl.loop(1, 16)
        def _(i):
            t = (pme + i) % 16
            to_owner(pme, t).wait_recv()

        total = plane_rx[0].astype(F32)
        for t in range(1, 16):
            total += plane_rx[t].astype(F32)
        z_rx[z] = total.astype(BF)

        @pl.when(loss_tile(pme))
        def _():
            z_rx[z] = split_round(total)

        @pl.loop(1, 8)
        def _(i):
            along_z((z + i) % 8, z).start()

        @pl.loop(1, 8)
        def _(i):
            t = (z + i) % 8
            along_z(t, t).wait_recv()

        total = z_rx[0].astype(F32)
        for t in range(1, 8):
            total += z_rx[t].astype(F32)
        fin[core, pme] = total.astype(BF)

        @pl.when(loss_tile(pme))
        def _():
            fin[core, pme] = split_round(total)


        @pl.loop(1, 16)
        def _(i):
            to_plane((pme + i) % 16, pme).start()

        to_core(core, pme).start()

    @pl.loop(1, 16)
    def _(i):
        t = (pme + 16 - i) % 16

        @pl.when(t < TILES)
        def _():
            to_plane(pme, t).wait_recv()
            to_core(core, t).start()

    @pl.loop(0, TILES)
    def _(t):
        to_core(1 - core, t).wait_recv()

    @pl.loop(1, 16)
    def _(i):
        t = (pme + i) % 16

        @pl.when(t < TILES)
        def _():
            to_owner(t, pme).wait_send()

    @pl.when(pme < TILES)
    def _():
        @pl.loop(1, 8)
        def _(i):
            along_z((z + i) % 8, z).wait_send()

        @pl.loop(1, 16)
        def _(i):
            to_plane((pme + i) % 16, pme).wait_send()

    @pl.loop(0, TILES)
    def _(t):
        to_core(core, t).wait_send()


def unpack(fin, sg_ref, score_ref, sg_out, gg_out, gc_out, sg_held, gg_held, gc_held, sem):
    copies = []

    def send(held, out):
        copies.append(pltpu.make_async_copy(held, out, sem.at[len(copies)]))
        copies[-1].start()

    root = 1.0 / math.sqrt(262144.0)
    for g, held, out, full_taps, half_tap in ((0, gc_held, gc_out, (2, 0), 1), (1, gg_held, gg_out, (1, 2), 0)):
        for n in range(9):
            first = (n // 3) * 9 + (1, 2, 0)[n % 3] * 3
            full = fin[g, n].astype(F32) * root
            held[first + full_taps[0]] = full[:, 0:64]
            held[first + full_taps[1]] = full[:, 64:128]
            half = fin[g, 9 + n // 2].astype(F32) * root
            held[first + half_tap] = half[:, 0:64] if n % 2 == 0 else half[:, 64:128]
            if n % 3 == 2:
                here = pl.ds((n // 3) * 9, 9)
                send(held.at[here], out.at[here])
    for r in range(8):
        sg_held[:, r, :] = sg_ref[r]
    send(sg_held, sg_out)
    loss = fin[0, 13].astype(F32)
    loss = loss[0:16] + loss[16:32] + loss[32:48]
    first = jnp.logical_and(lane((16, 128)) == 64, lax.broadcasted_iota(jnp.int32, (16, 128), 0) == 0)
    score_ref[0, 0] = jnp.sum(jnp.where(first, loss, 0.0)) * (1.0 / 262144.0)
    for copy in copies:
        copy.wait()


def shards(sources, generator_weight, critic_kernel_weight, readout, load_weight):
    vmem = pl.BlockSpec(memory_space=pltpu.VMEM)
    smem = pl.BlockSpec(memory_space=pltpu.SMEM)
    dma = pltpu.SemaphoreType.DMA
    hbm = pl.BlockSpec(memory_space=pltpu.HBM)
    source_gradient, taps = pl.pallas_call(
        kernel,
        out_shape=(
            pltpu.VMEM((8, 64, 128), F32),
            pltpu.VMEM((2, TILES, 64, 128), BF),
        ),
        in_specs=[hbm, hbm, hbm, hbm, smem],
        out_specs=(vmem, vmem),
        scratch_shapes=[
            pltpu.VMEM((64, 8, 128), BF),
            pltpu.VMEM((27, 64, 64), BF),
            pltpu.VMEM((27, 64, 64), BF),
            pltpu.VMEM((1, 64), F32),
            dma((4,)),
            pltpu.SemaphoreType.REGULAR((3,)),
            pltpu.VMEM((2, 256, LANES), F32),
            pltpu.VMEM((64, 8, 128), F32),
            pltpu.VMEM((3, 10, 64, 128), BF),
            pltpu.VMEM((3, 10, 64, 128), BF),
            pltpu.VMEM((3, 256, 256), BF),
            pltpu.VMEM((3, 256, 256), BF),
            pltpu.VMEM((3, 256, 256), BF),
            pltpu.VMEM((3, 256, 256), BF),
            pltpu.VMEM((3, 256, LANES), BF),
            pltpu.VMEM((3, 256, LANES), BF),
            pltpu.VMEM((3, 256, LANES), BF),
            pltpu.VMEM((3, 256, LANES), F32),
            pltpu.VMEM((3, 256, LANES), BF),
            pltpu.VMEM((256, LANES), F32),
            pltpu.VMEM((64, 128), F32),
            pltpu.VMEM((1, 256), F32),
            pltpu.VMEM((2, TILES, 64, 128), F32),
            pltpu.VMEM((TILES, 64, 128), F32),
            pltpu.VMEM((TILES, 64, 128), BF),
            pltpu.VMEM((16, 64, 128), BF),
            pltpu.VMEM((8, 64, 128), BF),
            dma((32,)), dma((32,)), dma((32,)), dma((32,)), dma((4,)), dma((4,)),
            dma((TILES,)), dma((16,)), dma((8,)), dma((8,)),
            dma((16,)), dma((TILES,)), dma((TILES,)), dma((TILES,)),
        ],
        compiler_params=pltpu.CompilerParams(
            collective_id=0, has_side_effects=True, vmem_limit_bytes=56 * 2**20
        ),
        cost_estimate=pl.CostEstimate(flops=3 * 10**9, bytes_accessed=4 * 10**6, transcendentals=2 * 10**6),
    )(
        sources.reshape(64, 8, 128),
        generator_weight.reshape(27, 64, 64),
        critic_kernel_weight.reshape(27, 64, 64),
        readout.reshape(1, 64),
        load_weight,
    )
    score, source_gradient, gen, crit = pl.pallas_call(
        unpack,
        out_shape=(
            jax.ShapeDtypeStruct((1, 1), F32),
            jax.ShapeDtypeStruct((64, 8, 128), F32),
            jax.ShapeDtypeStruct((27, 64, 64), F32),
            jax.ShapeDtypeStruct((27, 64, 64), F32),
        ),
        in_specs=[vmem, vmem],
        out_specs=(smem, hbm, hbm, hbm),
        scratch_shapes=[
            pltpu.VMEM((64, 8, 128), F32),
            pltpu.VMEM((27, 64, 64), F32),
            pltpu.VMEM((27, 64, 64), F32),
            dma((7,)),
        ],
        compiler_params=pltpu.CompilerParams(vmem_limit_bytes=16 * 2**20),
    )(taps, source_gradient)
    return (
        score.reshape(()),
        source_gradient.reshape(1, 64, 1, 8, 128),
        gen.reshape(3, 3, 3, 64, 64),
        crit.reshape(3, 3, 3, 64, 64),
    )


def solution(mesh):
    placed = (P(None, None, "gx", "gy", None), P(), P(), P(), P("gx", "gy"))
    return jax.shard_map(
        shards,
        mesh=mesh,
        in_specs=placed,
        out_specs=(P(), P(None, None, "gx", "gy", None), P(), P()),
        check_vma=False,
    )
```

```python
import math

import jax
import jax.numpy as jnp
from jax import lax
from jax.experimental import pallas as pl
from jax.experimental.pallas import tpu as pltpu
from jax.sharding import PartitionSpec as P

MESH = pl.DeviceIdType.MESH
BF = jnp.bfloat16
F32 = jnp.float32
ROWS = 9
LANES = ROWS * 128
TILES = 14
TAP = {(0, 0): 1, (1, 0): 2, (1, 1): 0}
SIDES = [(1, 0), (-1, 0), (0, 1), (0, -1), (1, 1), (1, -1), (-1, 1), (-1, -1)]


AWAY = sorted(
    ((a, b) for a in range(4) for b in range(4) if a or b),
    key=lambda step: -min(step[0], 4 - step[0]) - min(step[1], 4 - step[1]),
)
AWAY_Z = (4, 3, 5, 2, 6, 1, 7)


def dot(a, b):
    return lax.dot_general(a, b, (((1,), (0,)), ((), ())), preferred_element_type=F32)


def dot_t(a, b):
    return lax.dot_general(a, b, (((1,), (1,)), ((), ())), preferred_element_type=F32)


def lane(shape):
    return lax.broadcasted_iota(jnp.int32, shape, len(shape) - 1)


def next_z(value):
    moved = pltpu.roll(value, 127, 1)
    return jnp.where(lane(value.shape) < 127, moved, 0.0)


def prev_z(value):
    moved = pltpu.roll(value, 1, 1)
    return jnp.where(lane(value.shape) > 0, moved, 0.0)


def at(row, count=1):
    return pl.ds(pl.multiple_of(row * 128, 128), count * 128)


def split_round(value):
    plain = value.astype(BF)
    loss = value[0:16] + value[16:32] + value[32:48]
    high = loss.astype(BF)
    rest = loss - high.astype(F32)
    middle = rest.astype(BF)
    low = (rest - middle.astype(F32)).astype(BF)
    parts = jnp.concatenate([high, middle, low, jnp.zeros_like(high)], 0).astype(F32)
    return jnp.where(lane(value.shape) >= 64, parts, plain.astype(F32)).astype(BF)


def kernel(
    src_hbm, wg_hbm, wc_hbm, ro_hbm, lw_ref,
    sg_ref, fin,
    src_ref, wg_ref, wc_ref, ro_ref, lsem, rounds, half_field, stage, sbuf, dbuf, wg, wgt, wc, wct, u, d, f, slope, dg, q, ro, lossv,
    part, core_rx, psend, plane_rx, z_rx,
    s_s, s_r, d_s, d_r, c_s, c_r, p_s, p_r, z_s, z_r, g_s, g_r, f_s, f_r,
):
    gx, gy = lax.axis_index("gx"), lax.axis_index("gy")
    z, y, x, core = gx // 4, gx % 4, gy // 2, gy % 2
    pme = x * 4 + y

    def plane_dev(p):
        return (z * 4 + p % 4, (p // 4) * 2 + core)

    def z_dev(t):
        return (t * 4 + y, gy)

    core_dev = (gx, x * 2 + (1 - core))

    def side_dev(side):
        return ((gx + side[0] + 32) % 32, (gy + side[1] + 8) % 8)

    def rcopy(src, dst, send, recv, dev):
        return pltpu.make_async_remote_copy(
            src_ref=src, dst_ref=dst, send_sem=send, recv_sem=recv, device_id=dev, device_id_type=MESH
        )

    def halo(buf, n, send, recv, quarter=0):
        dx, dy = SIDES[n]
        if dy == 0:
            here = there = pl.ds(1 + 2 * quarter, 2)
        else:
            here, there = pl.ds(8 if dy > 0 else 1, 1), pl.ds(0 if dy > 0 else 9, 1)
        n = n + 8 * quarter
        return rcopy(buf.at[1, here], buf.at[1 - dx, there], send.at[n], recv.at[n], side_dev((dx, dy)))

    loads = [
        pltpu.make_async_copy(a, b, lsem.at[n])
        for n, (a, b) in enumerate(((src_hbm, src_ref), (wg_hbm, wg_ref), (wc_hbm, wc_ref), (ro_hbm, ro_ref)))
    ]
    for load in loads:
        load.start()

    barrier = pltpu.get_barrier_semaphore()

    def greet(dev):
        pl.semaphore_signal(barrier, inc=1, device_id=dev, device_id_type=MESH)

    for side in SIDES:
        greet(side_dev(side))
    greet(core_dev)

    near = [
        (gx, ((x + 1) % 4) * 2 + core),
        (gx, ((x + 3) % 4) * 2 + core),
        (z * 4 + (y + 1) % 4, gy),
        (z * 4 + (y + 3) % 4, gy),
        (((z + 1) % 8) * 4 + y, gy),
        (((z + 7) % 8) * 4 + y, gy),
    ]
    for dev in near:
        greet(dev)

    def tell(k):
        for dev in near:
            pl.semaphore_signal(rounds.at[k], inc=1, device_id=dev, device_id_type=MESH)

    def hear(k):
        pl.semaphore_wait(rounds.at[k], 6)

    loads[0].wait()
    stage[...] = src_ref[...].astype(F32)
    for r in range(8):
        sbuf[1, r + 1] = stage[:, r, :].astype(BF)

    pl.semaphore_wait(barrier, 8 + 1 + 6)
    parts = [(n, 0) for n in (4, 5, 6, 7, 2, 3)] + [(n, quarter) for quarter in range(4) for n in (0, 1)]
    for n, quarter in parts:
        halo(sbuf, n, s_s, s_r, quarter).start()
    tell(0)
    for load in loads[1:]:
        load.wait()

    zero = jnp.zeros((64, 64), F32)
    for s in range(3):
        for ay in range(2):
            for az in range(2):
                rows = pl.ds((ay * 2 + az) * 64, 64)
                for by in range(2):
                    pair = []
                    for bz in range(2):
                        ok = (by, ay) in TAP and (bz, az) in TAP
                        pair.append(wg_ref[s * 9 + TAP[by, ay] * 3 + TAP[bz, az]].astype(F32) if ok else zero)
                    wg[s, rows, pl.ds(by * 128, 128)] = jnp.concatenate(pair, 1).astype(BF)
                    pair = []
                    for bz in range(2):
                        ok = (ay, by) in TAP and (az, bz) in TAP
                        pair.append(wc_ref[s * 9 + TAP[ay, by] * 3 + TAP[az, bz]].astype(F32) if ok else zero)
                    wc[s, rows, pl.ds(by * 128, 128)] = jnp.concatenate(pair, 1).astype(BF)
        wgt[s] = wg[s].astype(F32).T.astype(BF)
        wct[s] = wc[s].astype(F32).T.astype(BF)
    ro[...] = jnp.broadcast_to(ro_ref[...], (128, 64)).T

    def spread(buf, out, xs, r, keep=None):
        value = buf[xs, r].astype(F32)
        if keep is not None:
            value = jnp.where(keep, value, 0.0)
        return value.astype(BF), next_z(value).astype(BF)

    def put_here(out, xs, r, pair):
        out[xs, 0:64, at(r)] = pair[0]
        out[xs, 64:128, at(r)] = pair[1]

    def put_below(out, xs, r, pair):
        out[xs, 128:192, at(r - 1)] = pair[0]
        out[xs, 192:256, at(r - 1)] = pair[1]

    def clear(out, xs):
        nothing = jnp.zeros((128, 128), BF)
        out[xs, 0:128, at(0)] = nothing
        out[xs, 128:256, at(8)] = nothing

    def own_rows(buf, out, xs, keep=None, first=1, last=8):
        @pl.loop(first, last + 1, unroll=min(4, last + 1 - first))
        def _(r):
            pair = spread(buf, out, xs, r, keep)
            put_here(out, xs, r, pair)
            put_below(out, xs, r, pair)

    def arrive(buf, out, send, recv, rest):
        for quarter in range(4):
            for n, xs, keep in ((0, 0, None), (1, 2, gx < 31)):
                halo(buf, n, send, recv, quarter).wait_recv()
                own_rows(buf, out, xs, keep, 2 * quarter + 1, 2 * quarter + 2)
            if quarter:
                rest(quarter - 1)
        for n in range(2, 8):
            halo(buf, n, send, recv).wait_recv()
        edge_rows(buf, out, 1)
        edge_rows(buf, out, 0)
        edge_rows(buf, out, 2, gx < 31)

    def edge_rows(buf, out, xs, keep=True):
        put_here(out, xs, 0, spread(buf, out, xs, 0, keep))
        put_below(out, xs, 9, spread(buf, out, xs, 9, jnp.logical_and(keep, gy < 7)))

    for xs in range(3):
        clear(u, xs)
        clear(d, xs)
    own_rows(sbuf, u, 1)

    def fire(s, v, c):
        t = jnp.tanh(0.5 * v)
        f[s, :, c] = (jnp.maximum(v, 0.2 * v) - 0.8 * jnp.log(1.0 + jnp.abs(t))).astype(BF)
        slope[s, :, c] = 0.6 + 0.4 * t

    def fire_low(s, v):
        t = jnp.tanh(0.5 * v)
        f[s, 128:256, 0:128] = (jnp.maximum(v, 0.2 * v) - 0.8 * jnp.log(1.0 + jnp.abs(t))).astype(BF)
        slope[s, 128:256, 0:128] = 0.6 + 0.4 * t

    def up_mid(weights, field, c):
        mid = field[1, :, c]
        return dot(weights[0], mid), dot(weights[1], mid), dot(weights[2], mid)

    def up_rest(weights, field, c):
        return dot(weights[2], field[0, :, c]), dot(weights[0], field[2, :, c])

    def up_low(weights, field):
        below, mid, above = field[0, :, 0:128], field[1, :, 0:128], field[2, :, 0:128]
        w0, w1, w2 = (weights[k, 128:256, :] for k in range(3))
        return dot(w2, below) + dot(w0, mid), dot(w1, mid), dot(w2, mid) + dot(w0, above)

    @pl.loop(0, 3)
    def _(j):
        c = at(j * 2 + 1, 2)
        low, mid, high = up_mid(wgt, u, c)
        fire(1, mid, c)
        slope[0, :, c] = low
        slope[2, :, c] = high

    for s in range(3):
        f[s, 0:128, 0:128] = jnp.zeros((128, 128), BF)
        dg[s, 0:128, 0:128] = jnp.zeros((128, 128), BF)

    def fire_rest(j):
        c = at(j * 2 + 1, 2)
        low, high = up_rest(wgt, u, c)
        fire(0, slope[0, :, c] + low, c)
        fire(2, slope[2, :, c] + high, c)

    arrive(sbuf, u, s_s, s_r, fire_rest)
    hear(0)
    tell(1)

    for s, v in enumerate(up_low(wgt, u)):
        fire_low(s, v)
    c = at(7, 2)
    low, mid, high = up_mid(wgt, u, c)
    fire(1, mid, c)
    slope[0, :, c] = low
    slope[2, :, c] = high

    fire_rest(3)

    @pl.when(gx == 0)
    def _():
        f[0] = jnp.zeros((256, LANES), BF)
        slope[0] = jnp.zeros((256, LANES), F32)

    @pl.when(gy == 0)
    def _():
        for s in range(3):
            f[s, 128:256, 0:128] = jnp.zeros((128, 128), BF)
            slope[s, 128:256, 0:128] = jnp.zeros((128, 128), F32)

    def down(weights, field, c):
        return dot(weights[0], field[0, :, c]) + dot(weights[1], field[1, :, c]) + dot(weights[2], field[2, :, c])

    def down_low(weights, field):
        terms = [dot(weights[k, 128:256, 128:256], field[k, 128:256, 0:128]) for k in range(3)]
        return terms[0] + terms[1] + terms[2]

    def gathered(r):
        near = q[0:64, at(r)] + q[128:192, at(r - 1)]
        far = q[64:128, at(r)] + q[192:256, at(r - 1)]
        return near + prev_z(far)

    q[128:256, 0:128] = down_low(wct, f)
    lossv[...] = jnp.zeros((1, 256), F32)

    def judge(r):
        near = q[0:64, at(r, 2)] + q[128:192, at(r - 1, 2)]
        far = q[64:128, at(r, 2)] + q[192:256, at(r - 1, 2)]
        v = near + jnp.where(lane((64, 256)) % 128 > 0, pltpu.roll(far, 1, 1), 0.0)
        t = jnp.tanh(0.5 * v)
        act = jnp.maximum(v, 0.2 * v) - 0.8 * jnp.log(1.0 + jnp.abs(t))
        read = jnp.concatenate([ro[...], ro[...]], 1)
        logits = jnp.sum(act * read, 0, keepdims=True)
        weight = jnp.where(lane((1, 256)) < 128, lw_ref[0, r - 1].astype(F32), lw_ref[0, r].astype(F32))
        e = jnp.exp(-jnp.abs(logits))
        lossv[...] += weight * (jnp.maximum(-logits, 0.0) + jnp.log1p(e))
        d_logit = -weight * jnp.where(logits >= 0, e, 1.0) / (1.0 + e)
        rows = (d_logit * read * (0.6 + 0.4 * t)).astype(BF)
        dbuf[1, r] = rows[:, 0:128]
        dbuf[1, r + 1] = rows[:, 128:256]

    for j in range(4):
        c = at(j * 2 + 1, 2)
        q[:, c] = down(wct, f, c)
        judge(2 * j + 1)
        for n in {0: (5, 7, 3), 3: (4, 6, 2)}.get(j, ()):
            halo(dbuf, n, d_s, d_r).start()
        for n in (0, 1):
            halo(dbuf, n, d_s, d_r, j).start()
    hear(1)
    tell(2)
    own_rows(dbuf, d, 1)

    @pl.loop(0, 3)
    def _(j):
        c = at(j * 2 + 1, 2)
        low, mid, high = up_mid(wc, d, c)
        dg[1, :, c] = (mid * slope[1, :, c]).astype(BF)
        half_field[0, :, c] = low
        half_field[1, :, c] = high

    def pair(g, k):
        lo, count = ((0, 3), (3, 3), (6, 3), (9, 5))[k]
        here = pl.ds(lo, count)
        return rcopy(part.at[g, here], core_rx.at[here], c_s.at[k], c_r.at[k], core_dev)

    def give(g, ks):
        @pl.when(core == 1 - g)
        def _():
            for k in ks:
                pair(g, k).start()

    def loss_tile(t):
        return jnp.logical_and(core == 0, t == 13)

    def other(step):
        return ((x + step[0]) % 4) * 4 + (y + step[1]) % 4

    def to_owner(dst, src):
        return rcopy(psend.at[dst], plane_rx.at[src], p_s.at[dst], p_r.at[src], plane_dev(dst))

    def begin_sum(g):
        @pl.when(core == g)
        def _():
            for k in range(4):
                pair(g, k).wait_recv()

            def ready(t):
                total = part[g, t] + core_rx[t]
                psend[t] = total.astype(BF)
                if g == 0:
                    @pl.when(t == 13)
                    def _():
                        psend[t] = split_round(total)

            for step in AWAY:
                t = other(step)

                @pl.when(t < TILES)
                def _():
                    ready(t)
                    to_owner(t, pme).start()

            @pl.when(pme < TILES)
            def _():
                ready(pme)

    def pack(g, s, full, halves):
        for j in range(3):
            n = s * 3 + j
            part[g, n] = full[j]
            left = lane((64, 128)) < 64
            half = halves[j]
            if (g == 0) == (n % 2 == 1):
                half = pltpu.roll(half, 64, 1)
            if n % 2 == 0:
                part[g, 9 + n // 2] = jnp.where(left, half, 0.0)
            else:
                part[g, 9 + n // 2] = jnp.where(left, part[g, 9 + n // 2], half)

    for s in range(3):
        q[:, 0:256] = dot_t(f[s], d[1])
        pairs = [(0, 0), (1, 0), (1, 1)]
        pack(
            0, s,
            [q[(p * 2 + 1) * 64:(p * 2 + 2) * 64, e * 128:e * 128 + 128] for p, e in pairs],
            [q[p * 128:p * 128 + 64, e * 128:e * 128 + 128] for p, e in pairs],
        )
        give(0, [s])
    loss = jnp.broadcast_to(jnp.sum(lossv[...], 1, keepdims=True), (16, 128))
    put = lane((16, 128)) >= 64
    part[0, 13, 0:16, :] = jnp.where(put, loss, part[0, 13, 0:16, :])
    give(0, [3])

    def back_rest(j):
        c = at(j * 2 + 1, 2)
        low, high = up_rest(wc, d, c)
        dg[0, :, c] = ((half_field[0, :, c] + low) * slope[0, :, c]).astype(BF)
        dg[2, :, c] = ((half_field[1, :, c] + high) * slope[2, :, c]).astype(BF)

    arrive(dbuf, d, d_s, d_r, back_rest)
    hear(2)
    begin_sum(0)

    for s, v in enumerate(up_low(wc, d)):
        dg[s, 128:256, 0:128] = (v * slope[s, 128:256, 0:128]).astype(BF)
    c = at(7, 2)
    low, mid, high = up_mid(wc, d, c)
    dg[1, :, c] = (mid * slope[1, :, c]).astype(BF)
    half_field[0, :, c] = low
    half_field[1, :, c] = high

    back_rest(3)

    clear(u, 1)
    for s in range(3):
        q[:, 0:256] = dot_t(u[1], dg[s])
        pairs = [(0, 0), (0, 1), (1, 1)]
        pack(
            1, s,
            [q[e * 128:e * 128 + 64, p * 128:p * 128 + 128] for e, p in pairs],
            [q[e * 128 + 64:e * 128 + 128, p * 128:p * 128 + 128] for e, p in pairs],
        )
        give(1, [s, 3] if s == 2 else [s])

    begin_sum(1)
    for n, quarter in parts:
        halo(sbuf, n, s_s, s_r, quarter).wait_send()
        halo(dbuf, n, d_s, d_r, quarter).wait_send()
    for k in range(4):
        pair(1 - core, k).wait_send()

    q[128:256, 0:128] = down_low(wg, dg)

    @pl.loop(0, 4)
    def _(j):
        c = at(j * 2 + 1, 2)
        q[:, c] = down(wg, dg, c)
        sg_ref[2 * j] = gathered(2 * j + 1)
        sg_ref[2 * j + 1] = gathered(2 * j + 2)

    def along_z(dst, src):
        return rcopy(z_rx.at[src], z_rx.at[src], z_s.at[dst], z_r.at[src], z_dev(dst))

    def to_plane(dst, src):
        return rcopy(fin.at[core, src], fin.at[core, src], g_s.at[dst], g_r.at[src], plane_dev(dst))

    def to_core(g, t):
        return rcopy(fin.at[g, t], fin.at[g, t], f_s.at[t], f_r.at[t], core_dev)

    @pl.when(pme < TILES)
    def _():
        plane_rx[pme] = psend[pme]

        @pl.loop(1, 16)
        def _(i):
            t = (pme + i) % 16
            to_owner(pme, t).wait_recv()

        total = plane_rx[0].astype(F32)
        for t in range(1, 16):
            total += plane_rx[t].astype(F32)
        z_rx[z] = total.astype(BF)

        @pl.when(loss_tile(pme))
        def _():
            z_rx[z] = split_round(total)

        for i in AWAY_Z:
            along_z((z + i) % 8, z).start()

        @pl.loop(1, 8)
        def _(i):
            t = (z + i) % 8
            along_z(t, t).wait_recv()

        total = z_rx[0].astype(F32)
        for t in range(1, 8):
            total += z_rx[t].astype(F32)
        fin[core, pme] = total.astype(BF)

        @pl.when(loss_tile(pme))
        def _():
            fin[core, pme] = split_round(total)


        for step in AWAY:
            to_plane(other(step), pme).start()

        to_core(core, pme).start()

    @pl.loop(1, 16)
    def _(i):
        t = (pme + 16 - i) % 16

        @pl.when(t < TILES)
        def _():
            to_plane(pme, t).wait_recv()
            to_core(core, t).start()

    @pl.loop(0, TILES)
    def _(t):
        to_core(1 - core, t).wait_recv()

    @pl.loop(1, 16)
    def _(i):
        t = (pme + i) % 16

        @pl.when(t < TILES)
        def _():
            to_owner(t, pme).wait_send()

    @pl.when(pme < TILES)
    def _():
        @pl.loop(1, 8)
        def _(i):
            along_z((z + i) % 8, z).wait_send()

        @pl.loop(1, 16)
        def _(i):
            to_plane((pme + i) % 16, pme).wait_send()

    @pl.loop(0, TILES)
    def _(t):
        to_core(core, t).wait_send()


def unpack(fin, sg_ref, score_ref, sg_out, gg_out, gc_out, sg_held, gg_held, gc_held, sem):
    copies = []

    def send(held, out):
        copies.append(pltpu.make_async_copy(held, out, sem.at[len(copies)]))
        copies[-1].start()

    root = 1.0 / math.sqrt(262144.0)
    for g, held, out, full_taps, half_tap in ((0, gc_held, gc_out, (2, 0), 1), (1, gg_held, gg_out, (1, 2), 0)):
        for n in range(9):
            first = (n // 3) * 9 + (1, 2, 0)[n % 3] * 3
            full = fin[g, n].astype(F32) * root
            held[first + full_taps[0]] = full[:, 0:64]
            held[first + full_taps[1]] = full[:, 64:128]
            half = fin[g, 9 + n // 2].astype(F32) * root
            held[first + half_tap] = half[:, 0:64] if n % 2 == 0 else half[:, 64:128]
            if n % 3 == 2:
                here = pl.ds((n // 3) * 9, 9)
                send(held.at[here], out.at[here])
    for r in range(8):
        sg_held[:, r, :] = sg_ref[r]
    send(sg_held, sg_out)
    loss = fin[0, 13].astype(F32)
    loss = loss[0:16] + loss[16:32] + loss[32:48]
    first = jnp.logical_and(lane((16, 128)) == 64, lax.broadcasted_iota(jnp.int32, (16, 128), 0) == 0)
    score_ref[0, 0] = jnp.sum(jnp.where(first, loss, 0.0)) * (1.0 / 262144.0)
    for copy in copies:
        copy.wait()


def shards(sources, generator_weight, critic_kernel_weight, readout, load_weight):
    vmem = pl.BlockSpec(memory_space=pltpu.VMEM)
    smem = pl.BlockSpec(memory_space=pltpu.SMEM)
    dma = pltpu.SemaphoreType.DMA
    hbm = pl.BlockSpec(memory_space=pltpu.HBM)
    source_gradient, taps = pl.pallas_call(
        kernel,
        out_shape=(
            pltpu.VMEM((8, 64, 128), F32),
            pltpu.VMEM((2, TILES, 64, 128), BF),
        ),
        in_specs=[hbm, hbm, hbm, hbm, smem],
        out_specs=(vmem, vmem),
        scratch_shapes=[
            pltpu.VMEM((64, 8, 128), BF),
            pltpu.VMEM((27, 64, 64), BF),
            pltpu.VMEM((27, 64, 64), BF),
            pltpu.VMEM((1, 64), F32),
            dma((4,)),
            pltpu.SemaphoreType.REGULAR((3,)),
            pltpu.VMEM((2, 256, LANES), F32),
            pltpu.VMEM((64, 8, 128), F32),
            pltpu.VMEM((3, 10, 64, 128), BF),
            pltpu.VMEM((3, 10, 64, 128), BF),
            pltpu.VMEM((3, 256, 256), BF),
            pltpu.VMEM((3, 256, 256), BF),
            pltpu.VMEM((3, 256, 256), BF),
            pltpu.VMEM((3, 256, 256), BF),
            pltpu.VMEM((3, 256, LANES), BF),
            pltpu.VMEM((3, 256, LANES), BF),
            pltpu.VMEM((3, 256, LANES), BF),
            pltpu.VMEM((3, 256, LANES), F32),
            pltpu.VMEM((3, 256, LANES), BF),
            pltpu.VMEM((256, LANES), F32),
            pltpu.VMEM((64, 128), F32),
            pltpu.VMEM((1, 256), F32),
            pltpu.VMEM((2, TILES, 64, 128), F32),
            pltpu.VMEM((TILES, 64, 128), F32),
            pltpu.VMEM((TILES, 64, 128), BF),
            pltpu.VMEM((16, 64, 128), BF),
            pltpu.VMEM((8, 64, 128), BF),
            dma((32,)), dma((32,)), dma((32,)), dma((32,)), dma((4,)), dma((4,)),
            dma((TILES,)), dma((16,)), dma((8,)), dma((8,)),
            dma((16,)), dma((TILES,)), dma((TILES,)), dma((TILES,)),
        ],
        compiler_params=pltpu.CompilerParams(
            collective_id=0, has_side_effects=True, vmem_limit_bytes=56 * 2**20
        ),
        cost_estimate=pl.CostEstimate(flops=3 * 10**9, bytes_accessed=4 * 10**6, transcendentals=2 * 10**6),
    )(
        sources.reshape(64, 8, 128),
        generator_weight.reshape(27, 64, 64),
        critic_kernel_weight.reshape(27, 64, 64),
        readout.reshape(1, 64),
        load_weight,
    )
    score, source_gradient, gen, crit = pl.pallas_call(
        unpack,
        out_shape=(
            jax.ShapeDtypeStruct((1, 1), F32),
            jax.ShapeDtypeStruct((64, 8, 128), F32),
            jax.ShapeDtypeStruct((27, 64, 64), F32),
            jax.ShapeDtypeStruct((27, 64, 64), F32),
        ),
        in_specs=[vmem, vmem],
        out_specs=(smem, hbm, hbm, hbm),
        scratch_shapes=[
            pltpu.VMEM((64, 8, 128), F32),
            pltpu.VMEM((27, 64, 64), F32),
            pltpu.VMEM((27, 64, 64), F32),
            dma((7,)),
        ],
        compiler_params=pltpu.CompilerParams(vmem_limit_bytes=16 * 2**20),
    )(taps, source_gradient)
    return (
        score.reshape(()),
        source_gradient.reshape(1, 64, 1, 8, 128),
        gen.reshape(3, 3, 3, 64, 64),
        crit.reshape(3, 3, 3, 64, 64),
    )


def solution(mesh):
    placed = (P(None, None, "gx", "gy", None), P(), P(), P(), P("gx", "gy"))
    return jax.shard_map(
        shards,
        mesh=mesh,
        in_specs=placed,
        out_specs=(P(), P(None, None, "gx", "gy", None), P(), P()),
        check_vma=False,
    )
```

```python
import math

import jax
import jax.numpy as jnp
from jax import lax
from jax.experimental import pallas as pl
from jax.experimental.pallas import tpu as pltpu
from jax.sharding import PartitionSpec as P

MESH = pl.DeviceIdType.MESH
BF = jnp.bfloat16
F32 = jnp.float32
ROWS = 9
LANES = ROWS * 128
TILES = 14
TAP = {(0, 0): 1, (1, 0): 2, (1, 1): 0}
SIDES = [(1, 0), (-1, 0), (0, 1), (0, -1), (1, 1), (1, -1), (-1, 1), (-1, -1)]


AWAY = sorted(
    ((a, b) for a in range(4) for b in range(4) if a or b),
    key=lambda step: -min(step[0], 4 - step[0]) - min(step[1], 4 - step[1]),
)
AWAY_Z = (4, 3, 5, 2, 6, 1, 7)


def dot(a, b):
    return lax.dot_general(a, b, (((1,), (0,)), ((), ())), preferred_element_type=F32)


def dot_t(a, b):
    return lax.dot_general(a, b, (((1,), (1,)), ((), ())), preferred_element_type=F32)


def lane(shape):
    return lax.broadcasted_iota(jnp.int32, shape, len(shape) - 1)


def next_z(value):
    moved = pltpu.roll(value, 127, 1)
    return jnp.where(lane(value.shape) < 127, moved, 0.0)


def prev_z(value):
    moved = pltpu.roll(value, 1, 1)
    return jnp.where(lane(value.shape) > 0, moved, 0.0)


def at(row, count=1):
    return pl.ds(pl.multiple_of(row * 128, 128), count * 128)


def split_round(value):
    plain = value.astype(BF)
    loss = value[0:16] + value[16:32] + value[32:48]
    high = loss.astype(BF)
    rest = loss - high.astype(F32)
    middle = rest.astype(BF)
    low = (rest - middle.astype(F32)).astype(BF)
    parts = jnp.concatenate([high, middle, low, jnp.zeros_like(high)], 0).astype(F32)
    return jnp.where(lane(value.shape) >= 64, parts, plain.astype(F32)).astype(BF)


def kernel(
    src_hbm, wg_hbm, wc_hbm, ro_hbm, lw_ref,
    sg_ref, fin,
    src_ref, wg_ref, wc_ref, ro_ref, lsem, rounds, half_field, stage, sbuf, dbuf, wg, wgt, wc, wct, u, d, f, slope, dg, q, ro, lossv,
    part, core_rx, psend, plane_rx, z_rx,
    s_s, s_r, d_s, d_r, c_s, c_r, p_s, p_r, z_s, z_r, g_s, g_r, f_s, f_r,
):
    gx, gy = lax.axis_index("gx"), lax.axis_index("gy")
    z, y, x, core = gx // 4, gx % 4, gy // 2, gy % 2
    pme = x * 4 + y

    def plane_dev(p):
        return (z * 4 + p % 4, (p // 4) * 2 + core)

    def z_dev(t):
        return (t * 4 + y, gy)

    core_dev = (gx, x * 2 + (1 - core))

    def side_dev(side):
        return ((gx + side[0] + 32) % 32, (gy + side[1] + 8) % 8)

    def rcopy(src, dst, send, recv, dev):
        return pltpu.make_async_remote_copy(
            src_ref=src, dst_ref=dst, send_sem=send, recv_sem=recv, device_id=dev, device_id_type=MESH
        )

    def halo(buf, n, send, recv, quarter=0):
        dx, dy = SIDES[n]
        if dy == 0:
            here = there = pl.ds(1 + 2 * quarter, 2)
        else:
            here, there = pl.ds(8 if dy > 0 else 1, 1), pl.ds(0 if dy > 0 else 9, 1)
        n = n + 8 * quarter
        return rcopy(buf.at[1, here], buf.at[1 - dx, there], send.at[n], recv.at[n], side_dev((dx, dy)))

    loads = [
        pltpu.make_async_copy(a, b, lsem.at[n])
        for n, (a, b) in enumerate(((src_hbm, src_ref), (wg_hbm, wg_ref), (wc_hbm, wc_ref), (ro_hbm, ro_ref)))
    ]
    for load in loads:
        load.start()

    barrier = pltpu.get_barrier_semaphore()

    def greet(dev):
        pl.semaphore_signal(barrier, inc=1, device_id=dev, device_id_type=MESH)

    for side in SIDES[4:] + SIDES[:4]:
        greet(side_dev(side))
    greet(core_dev)

    near = [
        (gx, ((x + 1) % 4) * 2 + core),
        (gx, ((x + 3) % 4) * 2 + core),
        (z * 4 + (y + 1) % 4, gy),
        (z * 4 + (y + 3) % 4, gy),
        (((z + 1) % 8) * 4 + y, gy),
        (((z + 7) % 8) * 4 + y, gy),
    ]
    for dev in near:
        greet(dev)

    def tell(k):
        for dev in near:
            pl.semaphore_signal(rounds.at[k], inc=1, device_id=dev, device_id_type=MESH)

    def hear(k):
        pl.semaphore_wait(rounds.at[k], 6)

    loads[0].wait()
    stage[...] = src_ref[...].astype(F32)
    for r in range(8):
        sbuf[1, r + 1] = stage[:, r, :].astype(BF)

    pl.semaphore_wait(barrier, 8 + 1 + 6)
    parts = [(n, 0) for n in (4, 5, 6, 7, 2, 3)] + [(n, quarter) for quarter in range(4) for n in (0, 1)]
    for n, quarter in parts:
        halo(sbuf, n, s_s, s_r, quarter).start()
    tell(0)
    for load in loads[1:]:
        load.wait()

    zero = jnp.zeros((64, 64), F32)
    for s in range(3):
        for ay in range(2):
            for az in range(2):
                rows = pl.ds((ay * 2 + az) * 64, 64)
                for by in range(2):
                    pair = []
                    for bz in range(2):
                        ok = (by, ay) in TAP and (bz, az) in TAP
                        pair.append(wg_ref[s * 9 + TAP[by, ay] * 3 + TAP[bz, az]].astype(F32) if ok else zero)
                    wg[s, rows, pl.ds(by * 128, 128)] = jnp.concatenate(pair, 1).astype(BF)
                    pair = []
                    for bz in range(2):
                        ok = (ay, by) in TAP and (az, bz) in TAP
                        pair.append(wc_ref[s * 9 + TAP[ay, by] * 3 + TAP[az, bz]].astype(F32) if ok else zero)
                    wc[s, rows, pl.ds(by * 128, 128)] = jnp.concatenate(pair, 1).astype(BF)
        wgt[s] = wg[s].astype(F32).T.astype(BF)
        wct[s] = wc[s].astype(F32).T.astype(BF)
    ro[...] = jnp.broadcast_to(ro_ref[...], (128, 64)).T

    def spread(buf, out, xs, r, keep=None):
        value = buf[xs, r].astype(F32)
        if keep is not None:
            value = jnp.where(keep, value, 0.0)
        return value.astype(BF), next_z(value).astype(BF)

    def put_here(out, xs, r, pair):
        out[xs, 0:64, at(r)] = pair[0]
        out[xs, 64:128, at(r)] = pair[1]

    def put_below(out, xs, r, pair):
        out[xs, 128:192, at(r - 1)] = pair[0]
        out[xs, 192:256, at(r - 1)] = pair[1]

    def clear(out, xs):
        nothing = jnp.zeros((128, 128), BF)
        out[xs, 0:128, at(0)] = nothing
        out[xs, 128:256, at(8)] = nothing

    def own_rows(buf, out, xs, keep=None, first=1, last=8):
        @pl.loop(first, last + 1, unroll=min(4, last + 1 - first))
        def _(r):
            pair = spread(buf, out, xs, r, keep)
            put_here(out, xs, r, pair)
            put_below(out, xs, r, pair)

    def arrive(buf, out, send, recv, rest):
        for quarter in range(4):
            for n, xs, keep in ((0, 0, None), (1, 2, gx < 31)):
                halo(buf, n, send, recv, quarter).wait_recv()
                own_rows(buf, out, xs, keep, 2 * quarter + 1, 2 * quarter + 2)
            if quarter:
                rest(quarter - 1)
        for n in range(2, 8):
            halo(buf, n, send, recv).wait_recv()
        edge_rows(buf, out, 1)
        edge_rows(buf, out, 0)
        edge_rows(buf, out, 2, gx < 31)

    def edge_rows(buf, out, xs, keep=True):
        put_here(out, xs, 0, spread(buf, out, xs, 0, keep))
        put_below(out, xs, 9, spread(buf, out, xs, 9, jnp.logical_and(keep, gy < 7)))

    for xs in range(3):
        clear(u, xs)
        clear(d, xs)
    own_rows(sbuf, u, 1)

    def fire(s, v, c):
        t = jnp.tanh(0.5 * v)
        f[s, :, c] = (jnp.maximum(v, 0.2 * v) - 0.8 * jnp.log(1.0 + jnp.abs(t))).astype(BF)
        slope[s, :, c] = 0.6 + 0.4 * t

    def fire_low(s, v):
        t = jnp.tanh(0.5 * v)
        f[s, 128:256, 0:128] = (jnp.maximum(v, 0.2 * v) - 0.8 * jnp.log(1.0 + jnp.abs(t))).astype(BF)
        slope[s, 128:256, 0:128] = 0.6 + 0.4 * t

    def up_mid(weights, field, c):
        mid = field[1, :, c]
        return dot(weights[0], mid), dot(weights[1], mid), dot(weights[2], mid)

    def up_rest(weights, field, c):
        return dot(weights[2], field[0, :, c]), dot(weights[0], field[2, :, c])

    def up_low(weights, field):
        below, mid, above = field[0, :, 0:128], field[1, :, 0:128], field[2, :, 0:128]
        w0, w1, w2 = (weights[k, 128:256, :] for k in range(3))
        return dot(w2, below) + dot(w0, mid), dot(w1, mid), dot(w2, mid) + dot(w0, above)

    @pl.loop(0, 3)
    def _(j):
        c = at(j * 2 + 1, 2)
        low, mid, high = up_mid(wgt, u, c)
        fire(1, mid, c)
        slope[0, :, c] = low
        slope[2, :, c] = high

    for s in range(3):
        f[s, 0:128, 0:128] = jnp.zeros((128, 128), BF)
        dg[s, 0:128, 0:128] = jnp.zeros((128, 128), BF)

    def fire_rest(j):
        c = at(j * 2 + 1, 2)
        low, high = up_rest(wgt, u, c)
        fire(0, slope[0, :, c] + low, c)
        fire(2, slope[2, :, c] + high, c)

    arrive(sbuf, u, s_s, s_r, fire_rest)
    hear(0)
    tell(1)

    for s, v in enumerate(up_low(wgt, u)):
        fire_low(s, v)
    c = at(7, 2)
    low, mid, high = up_mid(wgt, u, c)
    fire(1, mid, c)
    slope[0, :, c] = low
    slope[2, :, c] = high

    fire_rest(3)

    @pl.when(gx == 0)
    def _():
        f[0] = jnp.zeros((256, LANES), BF)
        slope[0] = jnp.zeros((256, LANES), F32)

    @pl.when(gy == 0)
    def _():
        for s in range(3):
            f[s, 128:256, 0:128] = jnp.zeros((128, 128), BF)
            slope[s, 128:256, 0:128] = jnp.zeros((128, 128), F32)

    def down(weights, field, c):
        return dot(weights[0], field[0, :, c]) + dot(weights[1], field[1, :, c]) + dot(weights[2], field[2, :, c])

    def down_low(weights, field):
        terms = [dot(weights[k, 128:256, 128:256], field[k, 128:256, 0:128]) for k in range(3)]
        return terms[0] + terms[1] + terms[2]

    def gathered(r):
        near = q[0:64, at(r)] + q[128:192, at(r - 1)]
        far = q[64:128, at(r)] + q[192:256, at(r - 1)]
        return near + prev_z(far)

    q[128:256, 0:128] = down_low(wct, f)
    lossv[...] = jnp.zeros((1, 256), F32)

    def judge(r):
        near = q[0:64, at(r, 2)] + q[128:192, at(r - 1, 2)]
        far = q[64:128, at(r, 2)] + q[192:256, at(r - 1, 2)]
        v = near + jnp.where(lane((64, 256)) % 128 > 0, pltpu.roll(far, 1, 1), 0.0)
        t = jnp.tanh(0.5 * v)
        act = jnp.maximum(v, 0.2 * v) - 0.8 * jnp.log(1.0 + jnp.abs(t))
        read = jnp.concatenate([ro[...], ro[...]], 1)
        logits = jnp.sum(act * read, 0, keepdims=True)
        weight = jnp.where(lane((1, 256)) < 128, lw_ref[0, r - 1].astype(F32), lw_ref[0, r].astype(F32))
        e = jnp.exp(-jnp.abs(logits))
        lossv[...] += weight * (jnp.maximum(-logits, 0.0) + jnp.log1p(e))
        d_logit = -weight * jnp.where(logits >= 0, e, 1.0) / (1.0 + e)
        rows = (d_logit * read * (0.6 + 0.4 * t)).astype(BF)
        dbuf[1, r] = rows[:, 0:128]
        dbuf[1, r + 1] = rows[:, 128:256]

    for j in range(4):
        c = at(j * 2 + 1, 2)
        q[:, c] = down(wct, f, c)
        judge(2 * j + 1)
        for n in {0: (5, 7, 3), 3: (4, 6, 2)}.get(j, ()):
            halo(dbuf, n, d_s, d_r).start()
        for n in (0, 1):
            halo(dbuf, n, d_s, d_r, j).start()
    hear(1)
    tell(2)
    own_rows(dbuf, d, 1)

    @pl.loop(0, 3)
    def _(j):
        c = at(j * 2 + 1, 2)
        low, mid, high = up_mid(wc, d, c)
        dg[1, :, c] = (mid * slope[1, :, c]).astype(BF)
        half_field[0, :, c] = low
        half_field[1, :, c] = high

    def pair(g, k):
        lo, count = ((0, 3), (3, 3), (6, 3), (9, 5))[k]
        here = pl.ds(lo, count)
        return rcopy(part.at[g, here], core_rx.at[here], c_s.at[k], c_r.at[k], core_dev)

    def give(g, ks):
        @pl.when(core == 1 - g)
        def _():
            for k in ks:
                pair(g, k).start()

    def loss_tile(t):
        return jnp.logical_and(core == 0, t == 13)

    def other(step):
        return ((x + step[0]) % 4) * 4 + (y + step[1]) % 4

    def to_owner(dst, src):
        return rcopy(psend.at[dst], plane_rx.at[src], p_s.at[dst], p_r.at[src], plane_dev(dst))

    def begin_sum(g):
        @pl.when(core == g)
        def _():
            for k in range(4):
                pair(g, k).wait_recv()

            def ready(t):
                total = part[g, t] + core_rx[t]
                psend[t] = total.astype(BF)
                if g == 0:
                    @pl.when(t == 13)
                    def _():
                        psend[t] = split_round(total)

            for step in AWAY:
                t = other(step)

                @pl.when(t < TILES)
                def _():
                    ready(t)
                    to_owner(t, pme).start()

            @pl.when(pme < TILES)
            def _():
                ready(pme)

    def pack(g, s, full, halves):
        for j in range(3):
            n = s * 3 + j
            part[g, n] = full[j]
            left = lane((64, 128)) < 64
            half = halves[j]
            if (g == 0) == (n % 2 == 1):
                half = pltpu.roll(half, 64, 1)
            if n % 2 == 0:
                part[g, 9 + n // 2] = jnp.where(left, half, 0.0)
            else:
                part[g, 9 + n // 2] = jnp.where(left, part[g, 9 + n // 2], half)

    for s in range(3):
        q[:, 0:256] = dot_t(f[s], d[1])
        pairs = [(0, 0), (1, 0), (1, 1)]
        pack(
            0, s,
            [q[(p * 2 + 1) * 64:(p * 2 + 2) * 64, e * 128:e * 128 + 128] for p, e in pairs],
            [q[p * 128:p * 128 + 64, e * 128:e * 128 + 128] for p, e in pairs],
        )
        give(0, [s])
    loss = jnp.broadcast_to(jnp.sum(lossv[...], 1, keepdims=True), (16, 128))
    put = lane((16, 128)) >= 64
    part[0, 13, 0:16, :] = jnp.where(put, loss, part[0, 13, 0:16, :])
    give(0, [3])

    def back_rest(j):
        c = at(j * 2 + 1, 2)
        low, high = up_rest(wc, d, c)
        dg[0, :, c] = ((half_field[0, :, c] + low) * slope[0, :, c]).astype(BF)
        dg[2, :, c] = ((half_field[1, :, c] + high) * slope[2, :, c]).astype(BF)

    arrive(dbuf, d, d_s, d_r, back_rest)
    hear(2)

    for s, v in enumerate(up_low(wc, d)):
        dg[s, 128:256, 0:128] = (v * slope[s, 128:256, 0:128]).astype(BF)
    c = at(7, 2)
    low, mid, high = up_mid(wc, d, c)
    dg[1, :, c] = (mid * slope[1, :, c]).astype(BF)
    half_field[0, :, c] = low
    half_field[1, :, c] = high

    back_rest(3)

    clear(u, 1)
    for s in range(3):
        q[:, 0:256] = dot_t(u[1], dg[s])
        pairs = [(0, 0), (0, 1), (1, 1)]
        pack(
            1, s,
            [q[e * 128:e * 128 + 64, p * 128:p * 128 + 128] for e, p in pairs],
            [q[e * 128 + 64:e * 128 + 128, p * 128:p * 128 + 128] for e, p in pairs],
        )
        give(1, [s, 3] if s == 2 else [s])

    begin_sum(0)
    begin_sum(1)
    for n, quarter in parts:
        halo(sbuf, n, s_s, s_r, quarter).wait_send()
        halo(dbuf, n, d_s, d_r, quarter).wait_send()
    for k in range(4):
        pair(1 - core, k).wait_send()

    q[128:256, 0:128] = down_low(wg, dg)

    @pl.loop(0, 4)
    def _(j):
        c = at(j * 2 + 1, 2)
        q[:, c] = down(wg, dg, c)
        sg_ref[2 * j] = gathered(2 * j + 1)
        sg_ref[2 * j + 1] = gathered(2 * j + 2)

    def along_z(dst, src):
        return rcopy(z_rx.at[src], z_rx.at[src], z_s.at[dst], z_r.at[src], z_dev(dst))

    def to_plane(dst, src):
        return rcopy(fin.at[core, src], fin.at[core, src], g_s.at[dst], g_r.at[src], plane_dev(dst))

    def to_core(g, t):
        return rcopy(fin.at[g, t], fin.at[g, t], f_s.at[t], f_r.at[t], core_dev)

    @pl.when(pme < TILES)
    def _():
        total = psend[pme].astype(F32)
        for step in AWAY[::-1]:
            t = other(step)
            to_owner(pme, t).wait_recv()
            total += plane_rx[t].astype(F32)
        z_rx[z] = total.astype(BF)

        @pl.when(loss_tile(pme))
        def _():
            z_rx[z] = split_round(total)

        for i in AWAY_Z:
            along_z((z + i) % 8, z).start()

        @pl.loop(1, 8)
        def _(i):
            t = (z + i) % 8
            along_z(t, t).wait_recv()

        total = z_rx[0].astype(F32)
        for t in range(1, 8):
            total += z_rx[t].astype(F32)
        fin[core, pme] = total.astype(BF)

        @pl.when(loss_tile(pme))
        def _():
            fin[core, pme] = split_round(total)


        for step in AWAY:
            to_plane(other(step), pme).start()

        to_core(core, pme).start()

    @pl.loop(1, 16)
    def _(i):
        t = (pme + 16 - i) % 16

        @pl.when(t < TILES)
        def _():
            to_plane(pme, t).wait_recv()
            to_core(core, t).start()

    @pl.loop(0, TILES)
    def _(t):
        to_core(1 - core, t).wait_recv()

    @pl.loop(1, 16)
    def _(i):
        t = (pme + i) % 16

        @pl.when(t < TILES)
        def _():
            to_owner(t, pme).wait_send()

    @pl.when(pme < TILES)
    def _():
        @pl.loop(1, 8)
        def _(i):
            along_z((z + i) % 8, z).wait_send()

        @pl.loop(1, 16)
        def _(i):
            to_plane((pme + i) % 16, pme).wait_send()

    @pl.loop(0, TILES)
    def _(t):
        to_core(core, t).wait_send()


def unpack(fin, sg_ref, score_ref, sg_out, gg_out, gc_out, sg_held, gg_held, gc_held, sem):
    copies = []

    def send(held, out):
        copies.append(pltpu.make_async_copy(held, out, sem.at[len(copies)]))
        copies[-1].start()

    root = 1.0 / math.sqrt(262144.0)
    for g, held, out, full_taps, half_tap in ((0, gc_held, gc_out, (2, 0), 1), (1, gg_held, gg_out, (1, 2), 0)):
        for n in range(9):
            first = (n // 3) * 9 + (1, 2, 0)[n % 3] * 3
            full = fin[g, n].astype(F32) * root
            held[first + full_taps[0]] = full[:, 0:64]
            held[first + full_taps[1]] = full[:, 64:128]
            half = fin[g, 9 + n // 2].astype(F32) * root
            held[first + half_tap] = half[:, 0:64] if n % 2 == 0 else half[:, 64:128]
            if n % 3 == 2:
                here = pl.ds((n // 3) * 9, 9)
                send(held.at[here], out.at[here])
    for r in range(8):
        sg_held[:, r, :] = sg_ref[r]
    send(sg_held, sg_out)
    loss = fin[0, 13].astype(F32)
    loss = loss[0:16] + loss[16:32] + loss[32:48]
    first = jnp.logical_and(lane((16, 128)) == 64, lax.broadcasted_iota(jnp.int32, (16, 128), 0) == 0)
    score_ref[0, 0] = jnp.sum(jnp.where(first, loss, 0.0)) * (1.0 / 262144.0)
    for copy in copies:
        copy.wait()


def shards(sources, generator_weight, critic_kernel_weight, readout, load_weight):
    vmem = pl.BlockSpec(memory_space=pltpu.VMEM)
    smem = pl.BlockSpec(memory_space=pltpu.SMEM)
    dma = pltpu.SemaphoreType.DMA
    hbm = pl.BlockSpec(memory_space=pltpu.HBM)
    source_gradient, taps = pl.pallas_call(
        kernel,
        out_shape=(
            pltpu.VMEM((8, 64, 128), F32),
            pltpu.VMEM((2, TILES, 64, 128), BF),
        ),
        in_specs=[hbm, hbm, hbm, hbm, smem],
        out_specs=(vmem, vmem),
        scratch_shapes=[
            pltpu.VMEM((64, 8, 128), BF),
            pltpu.VMEM((27, 64, 64), BF),
            pltpu.VMEM((27, 64, 64), BF),
            pltpu.VMEM((1, 64), F32),
            dma((4,)),
            pltpu.SemaphoreType.REGULAR((3,)),
            pltpu.VMEM((2, 256, LANES), F32),
            pltpu.VMEM((64, 8, 128), F32),
            pltpu.VMEM((3, 10, 64, 128), BF),
            pltpu.VMEM((3, 10, 64, 128), BF),
            pltpu.VMEM((3, 256, 256), BF),
            pltpu.VMEM((3, 256, 256), BF),
            pltpu.VMEM((3, 256, 256), BF),
            pltpu.VMEM((3, 256, 256), BF),
            pltpu.VMEM((3, 256, LANES), BF),
            pltpu.VMEM((3, 256, LANES), BF),
            pltpu.VMEM((3, 256, LANES), BF),
            pltpu.VMEM((3, 256, LANES), F32),
            pltpu.VMEM((3, 256, LANES), BF),
            pltpu.VMEM((256, LANES), F32),
            pltpu.VMEM((64, 128), F32),
            pltpu.VMEM((1, 256), F32),
            pltpu.VMEM((2, TILES, 64, 128), F32),
            pltpu.VMEM((TILES, 64, 128), F32),
            pltpu.VMEM((TILES, 64, 128), BF),
            pltpu.VMEM((16, 64, 128), BF),
            pltpu.VMEM((8, 64, 128), BF),
            dma((32,)), dma((32,)), dma((32,)), dma((32,)), dma((4,)), dma((4,)),
            dma((TILES,)), dma((16,)), dma((8,)), dma((8,)),
            dma((16,)), dma((TILES,)), dma((TILES,)), dma((TILES,)),
        ],
        compiler_params=pltpu.CompilerParams(
            collective_id=0, has_side_effects=True, vmem_limit_bytes=56 * 2**20
        ),
        cost_estimate=pl.CostEstimate(flops=3 * 10**9, bytes_accessed=4 * 10**6, transcendentals=2 * 10**6),
    )(
        sources.reshape(64, 8, 128),
        generator_weight.reshape(27, 64, 64),
        critic_kernel_weight.reshape(27, 64, 64),
        readout.reshape(1, 64),
        load_weight,
    )
    score, source_gradient, gen, crit = pl.pallas_call(
        unpack,
        out_shape=(
            jax.ShapeDtypeStruct((1, 1), F32),
            jax.ShapeDtypeStruct((64, 8, 128), F32),
            jax.ShapeDtypeStruct((27, 64, 64), F32),
            jax.ShapeDtypeStruct((27, 64, 64), F32),
        ),
        in_specs=[vmem, vmem],
        out_specs=(smem, hbm, hbm, hbm),
        scratch_shapes=[
            pltpu.VMEM((64, 8, 128), F32),
            pltpu.VMEM((27, 64, 64), F32),
            pltpu.VMEM((27, 64, 64), F32),
            dma((7,)),
        ],
        compiler_params=pltpu.CompilerParams(vmem_limit_bytes=16 * 2**20),
    )(taps, source_gradient)
    return (
        score.reshape(()),
        source_gradient.reshape(1, 64, 1, 8, 128),
        gen.reshape(3, 3, 3, 64, 64),
        crit.reshape(3, 3, 3, 64, 64),
    )


def solution(mesh):
    placed = (P(None, None, "gx", "gy", None), P(), P(), P(), P("gx", "gy"))
    return jax.shard_map(
        shards,
        mesh=mesh,
        in_specs=placed,
        out_specs=(P(), P(None, None, "gx", "gy", None), P(), P()),
        check_vma=False,
    )
```
